128 devices in a mesh: lev: 4 (over z), strip: 32 (over y, x, core).
Axes of the slice: x: 4, y: 4, z: 4, core: 2. Of those that a mesh axis runs over, the one named last changes fastest.
Arguments:
- zonal_current_grid: float32 [4, 1024, 4096], P('lev', 'strip'), may hold values from -6 to 6
- meridional_current_grid: float32 [4, 1024, 4096], P('lev', 'strip'), may hold values from -6 to 6
- thermal_anomaly: float32 [4, 1024, 4096], P('lev', 'strip'), may hold values from -6 to 6
- water_indicator: int32 [4, 1024, 4096], P('lev', 'strip'), may hold values from 0 to 1
- owner_slot_patch_number: int32 [128, 128, 8], P(('lev', 'strip')), may hold values from 0 to 511
- owner_slot_tally: int32 [128, 128], P(('lev', 'strip')), may hold values from 0 to 8, as said below
Outputs:
- samples: float32 [131072, 128], P(('lev', 'strip'))
The draws below stay inside these ranges and needn't reach their ends.
Inputs may be any that keep to these rules, and one draw needn't show every extreme that they name: `owner_slot_patch_number`: a tile index of the source device. `owner_slot_tally`: some owner receives 8 samples from every source.
All inputs are finite; a program needn't handle non-finite values.
Results may differ from the reference program's by a relative error of at most 0.000071.
Values sent between devices are 32-bit elements; how exact they have to be, the bound alone decides.
No kernel may reach another device: no remote copies, remote signals or barrier semaphores. Data moves between devices by JAX's collectives and lax.ppermute only.
A program may use at most 64 MiB of HBM per device.

```python
import jax
import jax.numpy as jnp
from jax import lax

COLS_DEV = 128
CAP = 8
VERTICAL_STEPS = 4
RANKS = 128
MERIDIAN_LINES = 1024
PARALLEL_LINES = 4096
TILES_DEV = 512
N_STRIP = 32


def draw_water_indicator(key, part):
    coarse_key = jax.random.fold_in(key, 101)
    island_key = jax.random.fold_in(key, 102)
    coarse = jax.random.randint(coarse_key, (VERTICAL_STEPS, MERIDIAN_LINES // 32, PARALLEL_LINES // 32), 0, 10)
    depth = jnp.arange(VERTICAL_STEPS).astype(jnp.int32)[:, None, None]
    land_coarse = (coarse < 3 + depth % 4).astype(jnp.int32)
    land_fine = jnp.repeat(jnp.repeat(land_coarse, 32, axis=1), 32, axis=2)
    islands = (jax.random.randint(island_key, (VERTICAL_STEPS, MERIDIAN_LINES, PARALLEL_LINES), 0, 12) == 0).astype(jnp.int32)
    return (1 - jnp.maximum(land_fine, islands)).astype(jnp.int32)


def draw_owner_slot_tally(key, part):
    base_key = jax.random.fold_in(key, 201)
    load_key = jax.random.fold_in(key, 202)
    owner_key = jax.random.fold_in(key, 203)
    base = jax.random.randint(base_key, (RANKS, RANKS), 0, CAP + 1)
    loads = jax.random.randint(load_key, (RANKS,), 1, 4)
    counts = jnp.minimum(CAP, base * loads[None, :] // 2)
    full_owner = jax.random.randint(owner_key, (), 0, RANKS)
    owners = jnp.arange(RANKS).astype(jnp.int32)[None, :]
    counts = jnp.where(owners == full_owner, CAP, counts)
    return counts.astype(jnp.int32)


def place_ends(entries, rng, low, high):
    dims = entries.shape
    index_at = [jax.random.randint(jax.random.fold_in(rng, axis), (), 0, dims[axis]) for axis in range(len(dims))]
    entries = entries.at[tuple(index_at)].set(low)
    longest = dims.index(max(dims))
    index_at[longest] = (index_at[longest] + 1) % dims[longest]
    return entries.at[tuple(index_at)].set(high)


def level_of(stream_key, dims, cuts, low, high):
    def one(dim, parts):
        draws = jax.random.uniform(jax.random.fold_in(jax.random.fold_in(stream_key, 6), dim), (parts,), jnp.float32, low / len(cuts), high / len(cuts))
        return jnp.repeat(jnp.exp(draws), dims[dim] // parts).reshape((-1,) + (1,) * (len(dims) - dim - 1))

    loudness = one(*cuts[0])
    for cut in cuts[1:]:
        loudness = loudness * one(*cut)
    return loudness


def gaussian(stream_key, dims, width, reach, split=(), held_as=jnp.bfloat16):
    values = jax.random.normal(stream_key, dims, jnp.float32) * width
    if len(split) > 0:
        values = level_of(stream_key, dims, split, -0.22, 0.18) * values
    return jnp.clip(values, min=-reach, max=reach).astype(held_as)


def setup_inputs(seed: int = 0) -> dict:
    key_of = jax.random.split(jax.random.key(seed), 7)
    zonal_current_grid = gaussian(key_of[0], (VERTICAL_STEPS, MERIDIAN_LINES, PARALLEL_LINES), 1.0, 6.0, ((0, 4), (1, 32)), jnp.float32)
    meridional_current_grid = gaussian(key_of[1], (VERTICAL_STEPS, MERIDIAN_LINES, PARALLEL_LINES), 1.0, 6.0, ((0, 4), (1, 32)), jnp.float32)
    thermal_anomaly = gaussian(key_of[2], (VERTICAL_STEPS, MERIDIAN_LINES, PARALLEL_LINES), 1.0, 6.0, ((0, 4), (1, 32)), jnp.float32)
    water_indicator = draw_water_indicator(jax.random.fold_in(key_of[6], 71), 0)
    owner_slot_patch_number = place_ends(jax.random.randint(key_of[4], (RANKS, RANKS, CAP), 0, TILES_DEV), jax.random.fold_in(key_of[4], 1), 0, TILES_DEV - 1).astype(jnp.int32)
    owner_slot_tally = draw_owner_slot_tally(jax.random.fold_in(key_of[6], 71), 0)
    return {"zonal_current_grid": zonal_current_grid, "meridional_current_grid": meridional_current_grid, "thermal_anomaly": thermal_anomaly, "water_indicator": water_indicator, "owner_slot_patch_number": owner_slot_patch_number, "owner_slot_tally": owner_slot_tally}


halfwidth = 20
spread_cells = 7.0
denominator_floor = 0.05


def filter_taps():
    offsets = jnp.arange(-halfwidth, halfwidth + 1).astype(jnp.float32)
    weights = jnp.exp(-offsets * offsets / (2.0 * spread_cells * spread_cells))
    return weights / jnp.sum(weights)


def forcing_terms(filtered):
    denominator = jnp.maximum(filtered[8], denominator_floor)
    east_bar = filtered[0] / denominator
    north_bar = filtered[1] / denominator
    heat_bar = filtered[2] / denominator
    return jnp.stack([
        east_bar, north_bar, heat_bar,
        filtered[3] / denominator - east_bar * east_bar,
        filtered[4] / denominator - east_bar * north_bar,
        filtered[5] / denominator - north_bar * north_bar,
        filtered[6] / denominator - east_bar * heat_bar,
        filtered[7] / denominator - north_bar * heat_bar])


def lone_level_slice(given_arrays):
    zonal_current, meridional_current, thermal_anomaly_grid, water_presence = given_arrays
    weights = filter_taps()
    water_flags = water_presence.astype(jnp.float32)
    planes = jnp.stack([
        water_flags * zonal_current, water_flags * meridional_current, water_flags * thermal_anomaly_grid,
        water_flags * zonal_current * zonal_current, water_flags * zonal_current * meridional_current,
        water_flags * meridional_current * meridional_current, water_flags * zonal_current * thermal_anomaly_grid,
        water_flags * meridional_current * thermal_anomaly_grid, water_flags])
    zonal_pass = jnp.zeros_like(planes)
    for offset in range(-halfwidth, halfwidth + 1):
        zonal_pass = zonal_pass + weights[offset + halfwidth] * jnp.roll(planes, offset, axis=2)
    zonal_pass = zonal_pass[:, :, ::4]
    rows_total = zonal_pass.shape[1]
    padded = jnp.pad(zonal_pass, ((0, 0), (halfwidth, halfwidth), (0, 0)))
    meridional = jnp.zeros_like(zonal_pass)
    for offset in range(-halfwidth, halfwidth + 1):
        start = halfwidth - offset
        meridional = meridional + weights[offset + halfwidth] * padded[:, start:start + rows_total, :]
    return forcing_terms(meridional[:, ::4, :])


def reference(zonal_current_grid, meridional_current_grid, thermal_anomaly, water_indicator, owner_slot_patch_number, owner_slot_tally):
    state_variables = lax.map(lone_level_slice, (zonal_current_grid, meridional_current_grid, thermal_anomaly, water_indicator))
    levels = state_variables.shape[0]
    grouped = state_variables.reshape(levels, 8, MERIDIAN_LINES // 16, 4, N_STRIP, COLS_DEV // 16, 4)
    tile_rows = grouped.transpose(0, 4, 2, 5, 1, 3, 6).reshape(RANKS, TILES_DEV, 128)
    picked = jnp.take_along_axis(tile_rows, owner_slot_patch_number.reshape(RANKS, RANKS * CAP, 1), axis=1)
    picked = picked.reshape(RANKS, RANKS, CAP, 128)
    slot_index = jnp.arange(CAP).astype(jnp.int32)
    kept_slots = slot_index[None, None, :] < owner_slot_tally[:, :, None]
    picked = jnp.where(kept_slots[..., None], picked, jnp.zeros_like(picked))
    return picked.transpose(1, 0, 2, 3).reshape(RANKS * RANKS * CAP, 128)
```

```python
import jax
import jax.numpy as jnp
import ml_dtypes
import numpy as np
from jax import lax
from jax.experimental import pallas as pl
from jax.experimental.pallas import tpu as pltpu
from jax.sharding import PartitionSpec as P

HALF = 20
SPREAD = 7.0
FLOOR = 0.05
ROWS = 32
COLS = 4096
STRIPS = 32
GROUPS = 5
SLAB = 48
VMEM_LIMIT = 40 * 1024 * 1024


def band(offsets):
    taps = np.arange(-HALF, HALF + 1).astype(np.float64)
    total = np.exp(-taps * taps / (2.0 * SPREAD * SPREAD)).sum()
    off = offsets.astype(np.float64)
    weights = np.exp(-off * off / (2.0 * SPREAD * SPREAD)) / total
    return np.where(np.abs(offsets) <= HALF, weights, 0.0).astype(np.float32)


def two_parts(matrix):
    high = matrix.astype(ml_dtypes.bfloat16)
    low = (matrix - high.astype(np.float32)).astype(ml_dtypes.bfloat16)
    return high, low


def zonal_matrix():
    lane = np.arange(128)
    target = ((lane // 4) % 4) * 128 + 4 * (4 * (lane // 16) + lane % 4)
    source = np.arange(768)[:, None] - 128
    return np.concatenate(two_parts(band(source - target[None, :])), axis=1)


def partial_row(a, g):
    if g < 4:
        return 4 * (g - 1) + a
    return {0: 12, 3: -5}.get(a)


def meridional_matrices():
    rows = np.arange(ROWS)
    full = np.zeros((4 * GROUPS * 8, 8 * ROWS), np.float32)
    wet = np.zeros((4 * 8, ROWS), np.float32)
    for a in range(4):
        for g in range(GROUPS):
            i = partial_row(a, g)
            if i is None:
                continue
            weights = band(4 * i - rows)
            wet[a * 8 + g] = weights
            for p in range(8):
                full[(a * GROUPS + g) * 8 + p, p * ROWS : (p + 1) * ROWS] = weights
    return np.concatenate(two_parts(full), axis=0), np.concatenate(two_parts(wet), axis=0)


def three_parts(x):
    first = x.astype(jnp.bfloat16)
    rest = x - first.astype(jnp.float32)
    second = rest.astype(jnp.bfloat16)
    third = (rest - second.astype(jnp.float32)).astype(jnp.bfloat16)
    return first, second, third


def dot(a, b):
    return jnp.dot(a, b, preferred_element_type=jnp.float32)


def swap_bit(zero, one, lane, stride):
    bit = (lane & stride) != 0
    return (
        jnp.where(bit, pltpu.roll(one, stride, 1), zero),
        jnp.where(bit, one, pltpu.roll(zero, 128 - stride, 1)),
    )


def filter_kernel(u_in, v_in, t_in, w_in, wz_ref, gm_ref, gw_ref, out_ref, ub, vb, tb, wb, parts, sems):
    order = [7, 0, 1, 2, 3, 4, 5, 6]
    copies = {}
    for c in order:
        here = pl.ds(512 * c, 512)
        for k, (src, dst) in enumerate(((u_in, ub), (v_in, vb), (t_in, tb), (w_in, wb))):
            copies[c, k] = pltpu.make_async_copy(src.at[:, here], dst.at[:, here], sems.at[k, c])
            copies[c, k].start()

    def make_planes(c):
        for k in range(4):
            copies[c, k].wait()
        for strip in range(4 * c, 4 * c + 4):
            here = slice(128 * strip, 128 * strip + 128)
            places = [slice(128 * strip + 128, 128 * strip + 256)]
            if strip == STRIPS - 1:
                places.append(slice(0, 128))
            if strip == 0:
                places.append(slice(COLS + 128, COLS + 256))
            u, v, t = ub[:, here], vb[:, here], tb[:, here]
            w = wb[:, here].astype(jnp.float32)
            wu, wv, wt = w * u, w * v, w * t
            fields = (wu, wv, wt, wu * u, wu * v, wv * v, wu * t, wv * t)
            for p, field in enumerate(fields):
                for n, part in enumerate(three_parts(field)):
                    for place in places:
                        parts[n, p * ROWS : (p + 1) * ROWS, place] = part
            for place in places:
                parts[0, 8 * ROWS : 9 * ROWS, place] = w.astype(jnp.bfloat16)

    lane = lax.broadcasted_iota(jnp.int32, (SLAB, 128), 1)

    def quad(q):
        window = slice(512 * q, 512 * q + 768)
        wz = wz_ref[...]
        z = dot(parts[1, : 8 * ROWS, window], wz)
        z = z + dot(parts[2, : 8 * ROWS, window], wz)
        z = z + dot(parts[0, : 8 * ROWS, window], wz)
        z = z[:, :128] + z[:, 128:]
        zw = dot(parts[0, 8 * ROWS :, window], wz)
        zw = zw[:, :128] + zw[:, 128:]

        def across(g_ref, x):
            m = g_ref.shape[0] // 2
            pieces = jnp.concatenate(three_parts(x), axis=1)
            y = dot(g_ref[:m], pieces)
            low = dot(g_ref[m:], pieces[:, :256])
            return (y[:, 256:] + low[:, 128:]) + (y[:, 128:256] + low[:, :128]) + y[:, :128]

        y = across(gm_ref, z)
        yw = across(gw_ref, zw)
        x = [jnp.concatenate([y[40 * a : 40 * a + 40], yw[8 * a : 8 * a + 8]], axis=0) for a in range(4)]
        x[0], x[1] = swap_bit(x[0], x[1], lane, 4)
        x[2], x[3] = swap_bit(x[2], x[3], lane, 4)
        x[0], x[2] = swap_bit(x[0], x[2], lane, 8)
        x[1], x[3] = swap_bit(x[1], x[3], lane, 8)
        for s in range(4):
            out_ref[4 * q + s] = x[s]

    make_planes(7)
    make_planes(0)
    for q in range(8):
        if q + 1 < 7:
            make_planes(q + 1)
        quad(q)


def filter_call(u, v, t, w):
    wz = zonal_matrix()
    gm, gw = meridional_matrices()
    anywhere = pl.BlockSpec(memory_space=pl.ANY)
    inside = pl.BlockSpec(memory_space=pltpu.VMEM)
    return pl.pallas_call(
        filter_kernel,
        out_shape=jax.ShapeDtypeStruct((STRIPS, SLAB, 128), jnp.float32),
        in_specs=[anywhere] * 4 + [inside] * 3,
        out_specs=inside,
        scratch_shapes=[
            pltpu.VMEM((ROWS, COLS), jnp.float32),
            pltpu.VMEM((ROWS, COLS), jnp.float32),
            pltpu.VMEM((ROWS, COLS), jnp.float32),
            pltpu.VMEM((ROWS, COLS), jnp.int32),
            pltpu.VMEM((3, 9 * ROWS, COLS + 256), jnp.bfloat16),
            pltpu.SemaphoreType.DMA((4, 8)),
        ],
        compiler_params=pltpu.CompilerParams(vmem_limit_bytes=VMEM_LIMIT),
        name="filter",
    )(u, v, t, w, jnp.asarray(wz), jnp.asarray(gm), jnp.asarray(gw))


def collect_kernel(r_ref, pick_ref, out_ref, q_scr, table):
    row = lax.broadcasted_iota(jnp.int32, (8, 128), 0)
    lane = lax.broadcasted_iota(jnp.int32, (8, 128), 1)
    a_of_lane = (lane // 4) % 4
    first_row = a_of_lane[:1] == 0
    last_row = a_of_lane[:1] == 3

    def gathered(s, half, rows_of, keep_first, keep_last):
        total = r_ref[s, rows_of(1 + half)]
        if half == 0:
            near, near_group, far, keep = s - 1, 3, s + 1, keep_last
        else:
            near, near_group, far, keep = s + 1, 0, s - 1, keep_first
        if 0 <= near < STRIPS:
            total = total + r_ref[near, rows_of(near_group)]
        if 0 <= far < STRIPS:
            total = total + jnp.where(keep, r_ref[far, rows_of(4)], 0.0)
        return total

    for s in range(STRIPS):
        for half in range(2):
            top = gathered(s, half, lambda g: slice(8 * g, 8 * g + 8), a_of_lane == 0, a_of_lane == 3)
            wet = gathered(s, half, lambda g: slice(40 + g, 41 + g), first_row, last_row)
            m = top * (1.0 / jnp.maximum(wet, FLOOR))
            u = jnp.broadcast_to(m[0:1], (8, 128))
            v = jnp.broadcast_to(m[1:2], (8, 128))
            t = jnp.broadcast_to(m[2:3], (8, 128))
            left = jnp.where(row < 3, 0.0, jnp.where((row == 5) | (row == 7), v, u))
            right = jnp.where(row == 3, u, jnp.where(row < 6, v, t))
            ti = 2 * s + half
            q_scr[8 * ti : 8 * ti + 8] = m - left * right

    for block in range(8):
        x = [q_scr[pl.ds(64 * block + q, 8, stride=8), :] for q in range(8)]
        for k in range(3):
            for i in range(8):
                if not i & (1 << k):
                    j = i | (1 << k)
                    x[i], x[j] = swap_bit(x[i], x[j], lane, 16 << k)
        rows = jnp.concatenate(x, axis=0)
        table[64 * block : 64 * block + 64] = jnp.concatenate(three_parts(rows), axis=1)

    for m in range(4):
        here = slice(256 * m, 256 * m + 256)
        picked = dot(pick_ref[here], table[...])
        out_ref[here] = (picked[:, :128] + picked[:, 128:256]) + picked[:, 256:]


def collect_call(blocks, pick):
    inside = pl.BlockSpec(memory_space=pltpu.VMEM)
    return pl.pallas_call(
        collect_kernel,
        out_shape=jax.ShapeDtypeStruct((pick.shape[0], 128), jnp.float32),
        in_specs=[inside] * 2,
        out_specs=inside,
        scratch_shapes=[
            pltpu.VMEM((512, 128), jnp.float32),
            pltpu.VMEM((512, 384), jnp.bfloat16),
        ],
        compiler_params=pltpu.CompilerParams(vmem_limit_bytes=VMEM_LIMIT),
        name="collect",
    )(blocks, pick)


def pick_matrix(patch, tally):
    ranks, capacity = patch.shape
    place = (patch // 64) * 64 + (patch % 8) * 8 + (patch // 8) % 8
    kept = jnp.arange(capacity)[None, :] < tally[:, None]
    place = jnp.where(kept, place, -1).reshape(ranks * capacity, 1)
    return (place == jnp.arange(512)[None, :]).astype(jnp.bfloat16)


def on_device(
    zonal_current_grid,
    meridional_current_grid,
    thermal_anomaly,
    water_indicator,
    owner_slot_patch_number,
    owner_slot_tally,
):
    ranks, capacity = owner_slot_patch_number.shape[1:]
    blocks = filter_call(zonal_current_grid[0], meridional_current_grid[0], thermal_anomaly[0], water_indicator[0])
    pick = pick_matrix(owner_slot_patch_number[0], owner_slot_tally[0])
    blocks = lax.all_to_all(blocks, "strip", split_axis=0, concat_axis=0, tiled=True)
    outgoing = collect_call(blocks, pick).reshape(ranks, capacity, 128)
    arrived = lax.all_to_all(outgoing, ("lev", "strip"), split_axis=0, concat_axis=0, tiled=True)
    return arrived.reshape(ranks * capacity, 128)


def solution(mesh):
    return jax.shard_map(
        on_device,
        mesh=mesh,
        in_specs=(
            P("lev", "strip", None),
            P("lev", "strip", None),
            P("lev", "strip", None),
            P("lev", "strip", None),
            P(("lev", "strip"), None, None),
            P(("lev", "strip"), None),
        ),
        out_specs=P(("lev", "strip"), None),
        check_vma=False,
    )
```

```python
import jax
import jax.numpy as jnp
import ml_dtypes
import numpy as np
from jax import lax
from jax.experimental import pallas as pl
from jax.experimental.pallas import tpu as pltpu
from jax.sharding import PartitionSpec as P

HALF = 20
SPREAD = 7.0
FLOOR = 0.05
ROWS = 32
COLS = 4096
STRIPS = 32
GROUPS = 5
SLAB = 48
QUADS = 8
ENDS = (2, 8)
VMEM_LIMIT = 62 * 1024 * 1024


def band(offsets):
    taps = np.arange(-HALF, HALF + 1).astype(np.float64)
    total = np.exp(-taps * taps / (2.0 * SPREAD * SPREAD)).sum()
    off = offsets.astype(np.float64)
    weights = np.exp(-off * off / (2.0 * SPREAD * SPREAD)) / total
    return np.where(np.abs(offsets) <= HALF, weights, 0.0).astype(np.float32)


def two_parts(matrix):
    high = matrix.astype(ml_dtypes.bfloat16)
    low = (matrix - high.astype(np.float32)).astype(ml_dtypes.bfloat16)
    return high, low


def zonal_matrices():
    lane = np.arange(128)
    strip = (lane // 4) % 4
    target = strip * 128 + 4 * (4 * (lane // 16) + lane % 4)
    source = np.arange(256)[:, None]
    left = band(source - np.where(strip == 3, target - 512, target)[None, :])
    right = band(source + 256 - np.where(strip == 0, target + 512, target)[None, :])
    return [np.concatenate(two_parts(m), axis=1) for m in (left, right)]


def partial_row(a, g):
    if g < 4:
        return 4 * (g - 1) + a
    return {0: 12, 3: -5}.get(a)


def meridional_matrices():
    rows = np.arange(ROWS)
    full = np.zeros((4 * GROUPS * 8, 8 * ROWS), np.float32)
    wet = np.zeros((4 * 8, ROWS), np.float32)
    for a in range(4):
        for g in range(GROUPS):
            i = partial_row(a, g)
            if i is None:
                continue
            weights = band(4 * i - rows)
            wet[a * 8 + g] = weights
            for p in range(8):
                full[(a * GROUPS + g) * 8 + p, p * ROWS : (p + 1) * ROWS] = weights
    return [np.concatenate([high] * 3 + [low], axis=1) for high, low in map(two_parts, (full, wet))]


def three_parts(x):
    first = x.astype(jnp.bfloat16)
    rest = x - first.astype(jnp.float32)
    second = rest.astype(jnp.bfloat16)
    third = (rest - second.astype(jnp.float32)).astype(jnp.bfloat16)
    return first, second, third


def dot(a, b):
    return jnp.dot(a, b, preferred_element_type=jnp.float32)


def swap_bit(zero, one, lane, stride):
    bit = (lane & stride) != 0
    return (
        jnp.where(bit, pltpu.roll(one, stride, 1), zero),
        jnp.where(bit, one, pltpu.roll(zero, 128 - stride, 1)),
    )


def filter_kernel(*refs):
    inputs, constants, out_hbm = refs[:4], refs[4:8], refs[8]
    held, consts, (parts, left, right, packed) = refs[9:13], refs[13:17], refs[17:21]
    in_sems, const_sems, out_sems = refs[21:]
    wl_ref, wr_ref, gm_ref, gw_ref = consts

    loads = {}
    starts = (0,) + ENDS[:-1]
    for c, (begin, end) in enumerate(zip(starts, ENDS)):
        here = pl.ds(512 * begin, 512 * (end - begin))
        for k in range(4):
            loads[c, k] = pltpu.make_async_copy(inputs[k].at[:, here], held[k].at[:, here], in_sems.at[k, c])
            loads[c, k].start()
        if c == 0:
            fixed = [pltpu.make_async_copy(a, b, const_sems.at[n]) for n, (a, b) in enumerate(zip(constants, consts))]
            for copy in fixed:
                copy.start()

    def make_planes(c):
        for strip in range(4 * starts[c], 4 * ENDS[c]):
            here = slice(128 * strip, 128 * strip + 128)
            u, v, t = [held[k][:, here] for k in range(3)]
            w = held[3][:, here].astype(jnp.float32)
            wu, wv, wt = w * u, w * v, w * t
            fields = (wu, wv, wt, wu * u, wu * v, wv * v, wu * t, wv * t)
            for p, field in enumerate(fields):
                for n, part in enumerate(three_parts(field)):
                    parts[n, p * ROWS : (p + 1) * ROWS, here] = part
            parts[0, 8 * ROWS :, here] = w.astype(jnp.bfloat16)

    def zonal(q):
        for w_ref, start, to in ((wl_ref, 0, left), (wr_ref, 256, right)):
            window = slice(512 * q + start, 512 * q + start + 256)
            w = w_ref[...]
            first = dot(parts[0, :, window], w)
            z = first[: 8 * ROWS] + dot(parts[1, : 8 * ROWS, window], w) + dot(parts[2, : 8 * ROWS, window], w)
            to[q, : 8 * ROWS] = z[:, :128] + z[:, 128:]
            to[q, 8 * ROWS :] = first[8 * ROWS :, :128] + first[8 * ROWS :, 128:]

    lane = lax.broadcasted_iota(jnp.int32, (SLAB, 128), 1)
    strip_of_lane = (lax.broadcasted_iota(jnp.int32, (9 * ROWS, 128), 1) // 4) % 4
    stores = []

    def meridional(pair):
        z = []
        for q in pair:
            from_left = jnp.where(strip_of_lane == 3, left[(q + 1) % QUADS], left[q])
            from_right = jnp.where(strip_of_lane == 0, right[(q - 1) % QUADS], right[q])
            z.append(from_left + from_right)
        z = jnp.concatenate(z, axis=1)

        def across(g_ref, x):
            first, second, third = three_parts(x)
            return dot(g_ref[...], jnp.concatenate([first, second, third, first], axis=0))

        y = across(gm_ref, z[: 8 * ROWS])
        yw = across(gw_ref, z[8 * ROWS :])
        for n, q in enumerate(pair):
            here = slice(128 * n, 128 * n + 128)
            x = [
                jnp.concatenate([y[40 * a : 40 * a + 40, here], yw[8 * a : 8 * a + 8, here]], axis=0)
                for a in range(4)
            ]
            x[0], x[1] = swap_bit(x[0], x[1], lane, 4)
            x[2], x[3] = swap_bit(x[2], x[3], lane, 4)
            x[0], x[2] = swap_bit(x[0], x[2], lane, 8)
            x[1], x[3] = swap_bit(x[1], x[3], lane, 8)
            for s in range(4):
                packed[4 * q + s] = x[s]
            here = pl.ds(4 * q, 4)
            stores.append(pltpu.make_async_copy(packed.at[here], out_hbm.at[here], out_sems.at[q]))
            stores[-1].start()

    ready = 1
    for c, (begin, end) in enumerate(zip(starts, ENDS)):
        for k in range(4):
            loads[c, k].wait()
        make_planes(c)
        if c == 0:
            for copy in fixed:
                copy.wait()
        for q in range(begin, end):
            zonal(q)
        while ready + 2 < end:
            meridional((ready, ready + 1))
            ready += 2
    meridional((7, 0))
    for copy in stores:
        copy.wait()


def filter_call(u, v, t, w):
    constants = zonal_matrices() + meridional_matrices()
    anywhere = pl.BlockSpec(memory_space=pl.ANY)
    return pl.pallas_call(
        filter_kernel,
        out_shape=jax.ShapeDtypeStruct((STRIPS, SLAB, 128), jnp.float32),
        in_specs=[anywhere] * 8,
        out_specs=anywhere,
        scratch_shapes=[pltpu.VMEM((ROWS, COLS), x.dtype) for x in (u, v, t, w)]
        + [pltpu.VMEM(x.shape, jnp.bfloat16) for x in constants]
        + [
            pltpu.VMEM((3, 9 * ROWS, COLS), jnp.bfloat16),
            pltpu.VMEM((QUADS, 9 * ROWS, 128), jnp.float32),
            pltpu.VMEM((QUADS, 9 * ROWS, 128), jnp.float32),
            pltpu.VMEM((STRIPS, SLAB, 128), jnp.float32),
            pltpu.SemaphoreType.DMA((4, len(ENDS))),
            pltpu.SemaphoreType.DMA((4,)),
            pltpu.SemaphoreType.DMA((QUADS,)),
        ],
        compiler_params=pltpu.CompilerParams(vmem_limit_bytes=VMEM_LIMIT),
        name="filter",
    )(u, v, t, w, *map(jnp.asarray, constants))


def collect_kernel(r_ref, pick_ref, out_ref, q_scr, table):
    row = lax.broadcasted_iota(jnp.int32, (8, 128), 0)
    lane = lax.broadcasted_iota(jnp.int32, (8, 128), 1)
    a_of_lane = (lane // 4) % 4
    first_row = a_of_lane[:1] == 0
    last_row = a_of_lane[:1] == 3

    def gathered(s, half, rows_of, keep_first, keep_last):
        total = r_ref[s, rows_of(1 + half)]
        if half == 0:
            near, near_group, far, keep = s - 1, 3, s + 1, keep_last
        else:
            near, near_group, far, keep = s + 1, 0, s - 1, keep_first
        if 0 <= near < STRIPS:
            total = total + r_ref[near, rows_of(near_group)]
        if 0 <= far < STRIPS:
            total = total + jnp.where(keep, r_ref[far, rows_of(4)], 0.0)
        return total

    for s in range(STRIPS):
        for half in range(2):
            top = gathered(s, half, lambda g: slice(8 * g, 8 * g + 8), a_of_lane == 0, a_of_lane == 3)
            wet = gathered(s, half, lambda g: slice(40 + g, 41 + g), first_row, last_row)
            m = top * (1.0 / jnp.maximum(wet, FLOOR))
            u = jnp.broadcast_to(m[0:1], (8, 128))
            v = jnp.broadcast_to(m[1:2], (8, 128))
            t = jnp.broadcast_to(m[2:3], (8, 128))
            left = jnp.where(row < 3, 0.0, jnp.where((row == 5) | (row == 7), v, u))
            right = jnp.where(row == 3, u, jnp.where(row < 6, v, t))
            ti = 2 * s + half
            q_scr[8 * ti : 8 * ti + 8] = m - left * right

    for block in range(8):
        x = [q_scr[pl.ds(64 * block + q, 8, stride=8), :] for q in range(8)]
        for k in range(3):
            for i in range(8):
                if not i & (1 << k):
                    j = i | (1 << k)
                    x[i], x[j] = swap_bit(x[i], x[j], lane, 16 << k)
        rows = jnp.concatenate(x, axis=0)
        table[64 * block : 64 * block + 64] = jnp.concatenate(three_parts(rows), axis=1)

    for m in range(4):
        here = slice(256 * m, 256 * m + 256)
        picked = dot(pick_ref[here], table[...])
        out_ref[here] = (picked[:, :128] + picked[:, 128:256]) + picked[:, 256:]


def collect_call(blocks, pick):
    inside = pl.BlockSpec(memory_space=pltpu.VMEM)
    return pl.pallas_call(
        collect_kernel,
        out_shape=jax.ShapeDtypeStruct((pick.shape[0], 128), jnp.float32),
        in_specs=[inside] * 2,
        out_specs=inside,
        scratch_shapes=[
            pltpu.VMEM((512, 128), jnp.float32),
            pltpu.VMEM((512, 384), jnp.bfloat16),
        ],
        compiler_params=pltpu.CompilerParams(vmem_limit_bytes=VMEM_LIMIT),
        name="collect",
    )(blocks, pick)


def pick_matrix(patch, tally):
    ranks, capacity = patch.shape
    place = (patch // 64) * 64 + (patch % 8) * 8 + (patch // 8) % 8
    kept = jnp.arange(capacity)[None, :] < tally[:, None]
    place = jnp.where(kept, place, -1).reshape(ranks * capacity, 1)
    return (place == jnp.arange(512)[None, :]).astype(jnp.bfloat16)


def on_device(
    zonal_current_grid,
    meridional_current_grid,
    thermal_anomaly,
    water_indicator,
    owner_slot_patch_number,
    owner_slot_tally,
):
    ranks, capacity = owner_slot_patch_number.shape[1:]
    blocks = filter_call(zonal_current_grid[0], meridional_current_grid[0], thermal_anomaly[0], water_indicator[0])
    pick = pick_matrix(owner_slot_patch_number[0], owner_slot_tally[0])
    blocks = lax.all_to_all(blocks, "strip", split_axis=0, concat_axis=0, tiled=True)
    outgoing = collect_call(blocks, pick).reshape(ranks, capacity, 128)
    arrived = lax.all_to_all(outgoing, ("lev", "strip"), split_axis=0, concat_axis=0, tiled=True)
    return arrived.reshape(ranks * capacity, 128)


def solution(mesh):
    return jax.shard_map(
        on_device,
        mesh=mesh,
        in_specs=(
            P("lev", "strip", None),
            P("lev", "strip", None),
            P("lev", "strip", None),
            P("lev", "strip", None),
            P(("lev", "strip"), None, None),
            P(("lev", "strip"), None),
        ),
        out_specs=P(("lev", "strip"), None),
        check_vma=False,
    )
```

```python
import jax
import jax.numpy as jnp
import ml_dtypes
import numpy as np
from jax import lax
from jax.experimental import pallas as pl
from jax.experimental.pallas import tpu as pltpu
from jax.sharding import PartitionSpec as P

HALF = 20
SPREAD = 7.0
FLOOR = 0.05
ROWS = 32
COLS = 4096
STRIPS = 32
GROUPS = 5
SLAB = 48
CHIPS = 16
MERGED = 64
QUADS = 8
ENDS = (2, 8)
FILTER_VMEM = 24 * 1024 * 1024
COLLECT_VMEM = 16 * 1024 * 1024


def band(offsets):
    taps = np.arange(-HALF, HALF + 1).astype(np.float64)
    total = np.exp(-taps * taps / (2.0 * SPREAD * SPREAD)).sum()
    off = offsets.astype(np.float64)
    weights = np.exp(-off * off / (2.0 * SPREAD * SPREAD)) / total
    return np.where(np.abs(offsets) <= HALF, weights, 0.0).astype(np.float32)


def two_parts(matrix):
    high = matrix.astype(ml_dtypes.bfloat16)
    low = (matrix - high.astype(np.float32)).astype(ml_dtypes.bfloat16)
    return high, low


def zonal_matrices():
    lane = np.arange(128)
    strip = (lane // 4) % 4
    target = strip * 128 + 4 * (4 * (lane // 16) + lane % 4)
    source = np.arange(256)[:, None]
    left = band(source - np.where(strip == 3, target - 512, target)[None, :])
    right = band(source + 256 - np.where(strip == 0, target + 512, target)[None, :])
    return [np.concatenate(two_parts(m), axis=1) for m in (left, right)]


def partial_row(a, g):
    if g < 4:
        return 4 * (g - 1) + a
    return {0: 12, 3: -5}.get(a)


def meridional_matrices():
    rows = np.arange(ROWS)
    full = np.zeros((4 * GROUPS * 8, 8 * ROWS), np.float32)
    wet = np.zeros((4 * 8, ROWS), np.float32)
    for a in range(4):
        for g in range(GROUPS):
            i = partial_row(a, g)
            if i is None:
                continue
            weights = band(4 * i - rows)
            wet[a * 8 + g] = weights
            for p in range(8):
                full[(a * GROUPS + g) * 8 + p, p * ROWS : (p + 1) * ROWS] = weights
    return [np.concatenate([high] * 3 + [low], axis=1) for high, low in map(two_parts, (full, wet))]


def three_parts(x):
    first = x.astype(jnp.bfloat16)
    rest = x - first.astype(jnp.float32)
    second = rest.astype(jnp.bfloat16)
    third = (rest - second.astype(jnp.float32)).astype(jnp.bfloat16)
    return first, second, third


def dot(a, b):
    return jnp.dot(a, b, preferred_element_type=jnp.float32)


def swap_bit(zero, one, lane, stride):
    bit = (lane & stride) != 0
    return (
        jnp.where(bit, pltpu.roll(one, stride, 1), zero),
        jnp.where(bit, one, pltpu.roll(zero, 128 - stride, 1)),
    )


def filter_kernel(*refs):
    inputs, constants, outs = refs[:4], refs[4:8], refs[8:10]
    held, consts, (parts, left, right) = refs[10:14], refs[14:18], refs[18:21]
    in_sems, const_sems = refs[21:]
    is_first = lax.rem(lax.axis_index("strip"), 2) == 0
    wl_ref, wr_ref, gm_ref, gw_ref = consts

    loads = {}
    starts = (0,) + ENDS[:-1]
    for c, (begin, end) in enumerate(zip(starts, ENDS)):
        here = pl.ds(512 * begin, 512 * (end - begin))
        for k in range(4):
            loads[c, k] = pltpu.make_async_copy(inputs[k].at[:, here], held[k].at[:, here], in_sems.at[k, c])
            loads[c, k].start()
        if c == 0:
            fixed = [pltpu.make_async_copy(a, b, const_sems.at[n]) for n, (a, b) in enumerate(zip(constants, consts))]
            for copy in fixed:
                copy.start()

    def make_planes(c):
        for strip in range(4 * starts[c], 4 * ENDS[c]):
            here = slice(128 * strip, 128 * strip + 128)
            u, v, t = [held[k][:, here] for k in range(3)]
            w = held[3][:, here].astype(jnp.float32)
            wu, wv, wt = w * u, w * v, w * t
            fields = (wu, wv, wt, wu * u, wu * v, wv * v, wu * t, wv * t)
            for p, field in enumerate(fields):
                for n, part in enumerate(three_parts(field)):
                    parts[n, p * ROWS : (p + 1) * ROWS, here] = part
            parts[0, 8 * ROWS :, here] = w.astype(jnp.bfloat16)

    def zonal(q):
        for w_ref, start, to in ((wl_ref, 0, left), (wr_ref, 256, right)):
            window = slice(512 * q + start, 512 * q + start + 256)
            w = w_ref[...]
            first = dot(parts[0, :, window], w)
            z = first[: 8 * ROWS] + dot(parts[1, : 8 * ROWS, window], w) + dot(parts[2, : 8 * ROWS, window], w)
            to[q, : 8 * ROWS] = z[:, :128] + z[:, 128:]
            to[q, 8 * ROWS :] = first[8 * ROWS :, :128] + first[8 * ROWS :, 128:]

    lane = lax.broadcasted_iota(jnp.int32, (SLAB, 128), 1)
    strip_of_lane = (lax.broadcasted_iota(jnp.int32, (9 * ROWS, 128), 1) // 4) % 4

    def meridional(pair):
        z = []
        for q in pair:
            from_left = jnp.where(strip_of_lane == 3, left[(q + 1) % QUADS], left[q])
            from_right = jnp.where(strip_of_lane == 0, right[(q - 1) % QUADS], right[q])
            z.append(from_left + from_right)
        z = jnp.concatenate(z, axis=1)

        def across(g_ref, x):
            first, second, third = three_parts(x)
            return dot(g_ref[...], jnp.concatenate([first, second, third, first], axis=0))

        y = across(gm_ref, z[: 8 * ROWS])
        yw = across(gw_ref, z[8 * ROWS :])
        for n, q in enumerate(pair):
            here = slice(128 * n, 128 * n + 128)
            x = [
                jnp.concatenate([y[40 * a : 40 * a + 40, here], yw[8 * a : 8 * a + 8, here]], axis=0)
                for a in range(4)
            ]
            x[0], x[1] = swap_bit(x[0], x[1], lane, 4)
            x[2], x[3] = swap_bit(x[2], x[3], lane, 4)
            x[0], x[2] = swap_bit(x[0], x[2], lane, 8)
            x[1], x[3] = swap_bit(x[1], x[3], lane, 8)
            for n in range(2):
                outs[0][2 * q + n] = jnp.where(is_first, x[2 * n], x[2 * n + 1])
                outs[1][2 * q + n] = jnp.where(is_first, x[2 * n + 1], x[2 * n])

    ready = 1
    for c, (begin, end) in enumerate(zip(starts, ENDS)):
        for k in range(4):
            loads[c, k].wait()
        make_planes(c)
        if c == 0:
            for copy in fixed:
                copy.wait()
        for q in range(begin, end):
            zonal(q)
        while ready + 2 < end:
            meridional((ready, ready + 1))
            ready += 2
    meridional((7, 0))


def filter_call(u, v, t, w):
    constants = zonal_matrices() + meridional_matrices()
    anywhere = pl.BlockSpec(memory_space=pl.ANY)
    u, v, t, w, *constants = [
        pltpu.with_memory_space_constraint(jnp.asarray(x), pltpu.HBM) for x in (u, v, t, w, *constants)
    ]
    return pl.pallas_call(
        filter_kernel,
        out_shape=[jax.ShapeDtypeStruct((CHIPS, SLAB, 128), jnp.float32)] * 2,
        in_specs=[anywhere] * 8,
        out_specs=[pl.BlockSpec(memory_space=pltpu.VMEM)] * 2,
        scratch_shapes=[pltpu.VMEM((ROWS, COLS), x.dtype) for x in (u, v, t, w)]
        + [pltpu.VMEM(x.shape, jnp.bfloat16) for x in constants]
        + [
            pltpu.VMEM((3, 9 * ROWS, COLS), jnp.bfloat16),
            pltpu.VMEM((QUADS, 9 * ROWS, 128), jnp.float32),
            pltpu.VMEM((QUADS, 9 * ROWS, 128), jnp.float32),
            pltpu.SemaphoreType.DMA((4, len(ENDS))),
            pltpu.SemaphoreType.DMA((4,)),
        ],
        compiler_params=pltpu.CompilerParams(vmem_limit_bytes=FILTER_VMEM),
        name="filter",
    )(u, v, t, w, *constants)


def lane_rows():
    return (lax.broadcasted_iota(jnp.int32, (8, 128), 1) // 4) % 4


def merge_kernel(mine, theirs, out):
    is_first = lax.rem(lax.axis_index("strip"), 2) == 0
    a = lane_rows()
    for chip in range(CHIPS):
        for rows, to, keep in ((lambda g: slice(8 * g, 8 * g + 8), 0, a), (lambda g: slice(40 + g, 41 + g), 56, a[:1])):
            x = [mine[chip, rows(g)] for g in range(GROUPS)]
            y = [theirs[chip, rows(g)] for g in range(GROUPS)]
            one = [jnp.where(is_first, p, q) for p, q in zip(x, y)]
            two = [jnp.where(is_first, q, p) for p, q in zip(x, y)]
            groups = (
                one[0],
                one[1] + jnp.where(keep == 3, two[4], 0.0),
                one[2] + two[0],
                one[3] + two[1],
                two[2] + jnp.where(keep == 0, one[4], 0.0),
                two[3],
                jnp.where(keep == 3, one[4], two[4] * jnp.where(keep == 0, 1.0, 0.0)),
            )
            for g, group in enumerate(groups):
                if to == 0:
                    out[chip, 8 * g : 8 * g + 8] = group
                else:
                    out[chip, to + g : to + g + 1] = group
        out[chip, MERGED - 1 : MERGED] = jnp.zeros((1, 128), jnp.float32)


def merge_call(mine, theirs):
    inside = pl.BlockSpec(memory_space=pltpu.VMEM)
    return pl.pallas_call(
        merge_kernel,
        out_shape=jax.ShapeDtypeStruct((CHIPS, MERGED, 128), jnp.float32),
        in_specs=[inside] * 2,
        out_specs=inside,
        compiler_params=pltpu.CompilerParams(vmem_limit_bytes=COLLECT_VMEM),
        name="merge",
    )(mine, theirs)


def collect_kernel(r_ref, pick_ref, out_ref, q_scr, table):
    row = lax.broadcasted_iota(jnp.int32, (8, 128), 0)
    lane = lax.broadcasted_iota(jnp.int32, (8, 128), 1)
    a = lane_rows()

    def gathered(chip, part, rows_of, keep):
        total = r_ref[chip, rows_of(1 + part)]
        other = chip - 1 if part < 2 else chip + 1
        if 0 <= other < CHIPS:
            group = (5, 6, 6, 0)[part]
            near = r_ref[other, rows_of(group)]
            if group == 6:
                near = jnp.where(keep == (0 if part == 1 else 3), near, 0.0)
            total = total + near
        return total

    for chip in range(CHIPS):
        for part in range(4):
            top = gathered(chip, part, lambda g: slice(8 * g, 8 * g + 8), a)
            wet = gathered(chip, part, lambda g: slice(56 + g, 57 + g), a[:1])
            m = top * (1.0 / jnp.maximum(wet, FLOOR))
            u = jnp.broadcast_to(m[0:1], (8, 128))
            v = jnp.broadcast_to(m[1:2], (8, 128))
            t = jnp.broadcast_to(m[2:3], (8, 128))
            left = jnp.where(row < 3, 0.0, jnp.where((row == 5) | (row == 7), v, u))
            right = jnp.where(row == 3, u, jnp.where(row < 6, v, t))
            ti = 4 * chip + part
            q_scr[8 * ti : 8 * ti + 8] = m - left * right

    for block in range(8):
        x = [q_scr[pl.ds(64 * block + q, 8, stride=8), :] for q in range(8)]
        for k in range(3):
            for i in range(8):
                if not i & (1 << k):
                    j = i | (1 << k)
                    x[i], x[j] = swap_bit(x[i], x[j], lane, 16 << k)
        rows = jnp.concatenate(x, axis=0)
        table[64 * block : 64 * block + 64] = jnp.concatenate(three_parts(rows), axis=1)

    for m in range(4):
        here = slice(256 * m, 256 * m + 256)
        picked = dot(pick_ref[here], table[...])
        out_ref[here] = (picked[:, :128] + picked[:, 128:256]) + picked[:, 256:]


def collect_call(blocks, pick):
    inside = pl.BlockSpec(memory_space=pltpu.VMEM)
    return pl.pallas_call(
        collect_kernel,
        out_shape=jax.ShapeDtypeStruct((pick.shape[0], 128), jnp.float32),
        in_specs=[inside] * 2,
        out_specs=inside,
        scratch_shapes=[
            pltpu.VMEM((512, 128), jnp.float32),
            pltpu.VMEM((512, 384), jnp.bfloat16),
        ],
        compiler_params=pltpu.CompilerParams(vmem_limit_bytes=COLLECT_VMEM),
        name="collect",
    )(blocks, pick)


def pick_matrix(patch, tally):
    ranks, capacity = patch.shape
    place = (patch // 64) * 64 + (patch % 8) * 8 + (patch // 8) % 8
    kept = jnp.arange(capacity)[None, :] < tally[:, None]
    place = jnp.where(kept, place, -1).reshape(ranks * capacity, 1)
    return (place == jnp.arange(512)[None, :]).astype(jnp.bfloat16)


def on_device(
    zonal_current_grid,
    meridional_current_grid,
    thermal_anomaly,
    water_indicator,
    owner_slot_patch_number,
    owner_slot_tally,
):
    ranks, capacity = owner_slot_patch_number.shape[1:]
    mine, theirs = filter_call(zonal_current_grid[0], meridional_current_grid[0], thermal_anomaly[0], water_indicator[0])
    theirs = lax.ppermute(theirs, "strip", [(i, i ^ 1) for i in range(STRIPS)])
    blocks = merge_call(mine, theirs)
    pick = pick_matrix(owner_slot_patch_number[0], owner_slot_tally[0])
    blocks, pick = lax.optimization_barrier((blocks, pick))
    same_core = [list(range(core, STRIPS, 2)) for core in range(2)]
    blocks = lax.all_to_all(blocks, "strip", split_axis=0, concat_axis=0, axis_index_groups=same_core, tiled=True)
    outgoing = collect_call(blocks, pick).reshape(ranks, capacity, 128)
    arrived = lax.all_to_all(outgoing, ("lev", "strip"), split_axis=0, concat_axis=0, tiled=True)
    return arrived.reshape(ranks * capacity, 128)


def solution(mesh):
    return jax.shard_map(
        on_device,
        mesh=mesh,
        in_specs=(
            P("lev", "strip", None),
            P("lev", "strip", None),
            P("lev", "strip", None),
            P("lev", "strip", None),
            P(("lev", "strip"), None, None),
            P(("lev", "strip"), None),
        ),
        out_specs=P(("lev", "strip"), None),
        check_vma=False,
    )
```

```python
import jax
import jax.numpy as jnp
import ml_dtypes
import numpy as np
from jax import lax
from jax.experimental import pallas as pl
from jax.experimental.pallas import tpu as pltpu
from jax.sharding import PartitionSpec as P

HALF = 20
SPREAD = 7.0
FLOOR = 0.05
ROWS = 32
COLS = 4096
STRIPS = 32
GROUPS = 5
SLAB = 48
CHIPS = 16
MERGED = 64
QUADS = 8
ENDS = (1, 8)
FILTER_VMEM = 24 * 1024 * 1024
COLLECT_VMEM = 16 * 1024 * 1024


def band(offsets):
    taps = np.arange(-HALF, HALF + 1).astype(np.float64)
    total = np.exp(-taps * taps / (2.0 * SPREAD * SPREAD)).sum()
    off = offsets.astype(np.float64)
    weights = np.exp(-off * off / (2.0 * SPREAD * SPREAD)) / total
    return np.where(np.abs(offsets) <= HALF, weights, 0.0).astype(np.float32)


def two_parts(matrix):
    high = matrix.astype(ml_dtypes.bfloat16)
    low = (matrix - high.astype(np.float32)).astype(ml_dtypes.bfloat16)
    return high, low


def zonal_matrices():
    lane = np.arange(128)
    strip = (lane // 4) % 4
    target = strip * 128 + 4 * (4 * (lane // 16) + lane % 4)
    source = np.arange(256)[:, None]
    left = band(source - np.where(strip == 3, target - 512, target)[None, :])
    right = band(source + 256 - np.where(strip == 0, target + 512, target)[None, :])
    return [np.concatenate(two_parts(m), axis=1) for m in (left, right)]


def partial_row(a, g):
    if g < 4:
        return 4 * (g - 1) + a
    return {0: 12, 3: -5}.get(a)


def meridional_matrices():
    rows = np.arange(ROWS)
    full = np.zeros((4 * GROUPS * 8, 8 * ROWS), np.float32)
    wet = np.zeros((4 * 8, ROWS), np.float32)
    for a in range(4):
        for g in range(GROUPS):
            i = partial_row(a, g)
            if i is None:
                continue
            weights = band(4 * i - rows)
            wet[a * 8 + g] = weights
            for p in range(8):
                full[(a * GROUPS + g) * 8 + p, p * ROWS : (p + 1) * ROWS] = weights
    return [np.concatenate(two_parts(m), axis=1) for m in (full, wet)]


def three_parts(x):
    first = x.astype(jnp.bfloat16)
    rest = x - first.astype(jnp.float32)
    second = rest.astype(jnp.bfloat16)
    third = (rest - second.astype(jnp.float32)).astype(jnp.bfloat16)
    return first, second, third


def dot(a, b):
    return jnp.dot(a, b, preferred_element_type=jnp.float32)


def swap_bit(zero, one, lane, stride):
    bit = (lane & stride) != 0
    return (
        jnp.where(bit, pltpu.roll(one, stride, 1), zero),
        jnp.where(bit, one, pltpu.roll(zero, 128 - stride, 1)),
    )


def filter_kernel(*refs):
    inputs, constants, outs = refs[:4], refs[4:8], refs[8:10]
    held, consts, (parts, left, right) = refs[10:14], refs[14:18], refs[18:21]
    in_sems, const_sems = refs[21:]
    is_first = lax.rem(lax.axis_index("strip"), 2) == 0
    wl_ref, wr_ref, gm_ref, gw_ref = consts

    loads = {}
    starts = (0,) + ENDS[:-1]
    for c, (begin, end) in enumerate(zip(starts, ENDS)):
        here = pl.ds(512 * begin, 512 * (end - begin))
        for k in range(4):
            loads[c, k] = pltpu.make_async_copy(inputs[k].at[:, here], held[k].at[:, here], in_sems.at[k, c])
            loads[c, k].start()
        if c == 0:
            fixed = [pltpu.make_async_copy(a, b, const_sems.at[n]) for n, (a, b) in enumerate(zip(constants, consts))]
            for copy in fixed:
                copy.start()

    def make_planes(c):
        for strip in range(4 * starts[c], 4 * ENDS[c]):
            here = slice(128 * strip, 128 * strip + 128)
            u, v, t = [held[k][:, here] for k in range(3)]
            w = held[3][:, here].astype(jnp.float32)
            wu, wv, wt = w * u, w * v, w * t
            fields = (wu, wv, wt, wu * u, wu * v, wv * v, wu * t, wv * t)
            for p, field in enumerate(fields):
                for n, part in enumerate(three_parts(field)[: 3 if p < 3 else 2]):
                    parts[n, p * ROWS : (p + 1) * ROWS, here] = part
            parts[0, 8 * ROWS :, here] = w.astype(jnp.bfloat16)

    def zonal(q):
        for w_ref, start, to in ((wl_ref, 0, left), (wr_ref, 256, right)):
            window = slice(512 * q + start, 512 * q + start + 256)
            w = w_ref[...]
            first = dot(parts[0, :, window], w)
            z = first[: 8 * ROWS] + dot(parts[1, : 8 * ROWS, window], w)
            z = z[:, :128] + z[:, 128:]
            third = dot(parts[2, : 3 * ROWS, window], w[:, :128])
            to[q, : 3 * ROWS] = z[: 3 * ROWS] + third
            to[q, 3 * ROWS : 8 * ROWS] = z[3 * ROWS :]
            to[q, 8 * ROWS :] = first[8 * ROWS :, :128] + first[8 * ROWS :, 128:]

    lane = lax.broadcasted_iota(jnp.int32, (SLAB, 128), 1)
    strip_of_lane = (lax.broadcasted_iota(jnp.int32, (9 * ROWS, 128), 1) // 4) % 4

    def meridional(pair):
        z = []
        for q in pair:
            from_left = jnp.where(strip_of_lane == 3, left[(q + 1) % QUADS], left[q])
            from_right = jnp.where(strip_of_lane == 0, right[(q - 1) % QUADS], right[q])
            z.append(from_left + from_right)
        z = jnp.concatenate(z, axis=1)

        def across(g_ref, x):
            first, second, third = three_parts(x)
            depth = x.shape[0]
            high, low = g_ref[:, :depth], g_ref[:, depth:]
            return dot(high, third) + dot(low, first) + dot(high, second) + dot(high, first)

        y = across(gm_ref, z[: 8 * ROWS])
        yw = across(gw_ref, z[8 * ROWS :])
        for n, q in enumerate(pair):
            here = slice(128 * n, 128 * n + 128)
            x = [
                jnp.concatenate([y[40 * a : 40 * a + 40, here], yw[8 * a : 8 * a + 8, here]], axis=0)
                for a in range(4)
            ]
            x[0], x[1] = swap_bit(x[0], x[1], lane, 4)
            x[2], x[3] = swap_bit(x[2], x[3], lane, 4)
            x[0], x[2] = swap_bit(x[0], x[2], lane, 8)
            x[1], x[3] = swap_bit(x[1], x[3], lane, 8)
            for n in range(2):
                outs[0][2 * q + n] = jnp.where(is_first, x[2 * n], x[2 * n + 1])
                outs[1][2 * q + n] = jnp.where(is_first, x[2 * n + 1], x[2 * n])

    ready = 1
    for c, (begin, end) in enumerate(zip(starts, ENDS)):
        for k in range(4):
            loads[c, k].wait()
        make_planes(c)
        if c == 0:
            for copy in fixed:
                copy.wait()
        for q in range(begin, end):
            zonal(q)
        while ready + 2 < end:
            meridional((ready, ready + 1))
            ready += 2
    meridional((7, 0))


def filter_call(u, v, t, w):
    constants = zonal_matrices() + meridional_matrices()
    anywhere = pl.BlockSpec(memory_space=pl.ANY)
    u, v, t, w, *constants = [
        pltpu.with_memory_space_constraint(jnp.asarray(x), pltpu.HBM) for x in (u, v, t, w, *constants)
    ]
    return pl.pallas_call(
        filter_kernel,
        out_shape=[jax.ShapeDtypeStruct((CHIPS, SLAB, 128), jnp.float32)] * 2,
        in_specs=[anywhere] * 8,
        out_specs=[pl.BlockSpec(memory_space=pltpu.VMEM)] * 2,
        scratch_shapes=[pltpu.VMEM((ROWS, COLS), x.dtype) for x in (u, v, t, w)]
        + [pltpu.VMEM(x.shape, jnp.bfloat16) for x in constants]
        + [
            pltpu.VMEM((3, 9 * ROWS, COLS), jnp.bfloat16),
            pltpu.VMEM((QUADS, 9 * ROWS, 128), jnp.float32),
            pltpu.VMEM((QUADS, 9 * ROWS, 128), jnp.float32),
            pltpu.SemaphoreType.DMA((4, len(ENDS))),
            pltpu.SemaphoreType.DMA((4,)),
        ],
        compiler_params=pltpu.CompilerParams(vmem_limit_bytes=FILTER_VMEM),
        name="filter",
    )(u, v, t, w, *constants)


def lane_rows():
    return (lax.broadcasted_iota(jnp.int32, (8, 128), 1) // 4) % 4


def merge_kernel(mine, theirs, out):
    is_first = lax.rem(lax.axis_index("strip"), 2) == 0
    a = lane_rows()
    for chip in range(CHIPS):
        for rows, to, keep in ((lambda g: slice(8 * g, 8 * g + 8), 0, a), (lambda g: slice(40 + g, 41 + g), 56, a[:1])):
            x = [mine[chip, rows(g)] for g in range(GROUPS)]
            y = [theirs[chip, rows(g)] for g in range(GROUPS)]
            one = [jnp.where(is_first, p, q) for p, q in zip(x, y)]
            two = [jnp.where(is_first, q, p) for p, q in zip(x, y)]
            groups = (
                one[0],
                one[1] + jnp.where(keep == 3, two[4], 0.0),
                one[2] + two[0],
                one[3] + two[1],
                two[2] + jnp.where(keep == 0, one[4], 0.0),
                two[3],
                jnp.where(keep == 3, one[4], two[4] * jnp.where(keep == 0, 1.0, 0.0)),
            )
            for g, group in enumerate(groups):
                if to == 0:
                    out[chip, 8 * g : 8 * g + 8] = group
                else:
                    out[chip, to + g : to + g + 1] = group
        out[chip, MERGED - 1 : MERGED] = jnp.zeros((1, 128), jnp.float32)


def merge_call(mine, theirs):
    inside = pl.BlockSpec(memory_space=pltpu.VMEM)
    return pl.pallas_call(
        merge_kernel,
        out_shape=jax.ShapeDtypeStruct((CHIPS, MERGED, 128), jnp.float32),
        in_specs=[inside] * 2,
        out_specs=inside,
        compiler_params=pltpu.CompilerParams(vmem_limit_bytes=COLLECT_VMEM),
        name="merge",
    )(mine, theirs)


def collect_kernel(r_ref, pick_ref, out_ref, q_scr, table):
    row = lax.broadcasted_iota(jnp.int32, (8, 128), 0)
    lane = lax.broadcasted_iota(jnp.int32, (8, 128), 1)
    a = lane_rows()

    def gathered(chip, part, rows_of, keep):
        total = r_ref[chip, rows_of(1 + part)]
        other = chip - 1 if part < 2 else chip + 1
        if 0 <= other < CHIPS:
            group = (5, 6, 6, 0)[part]
            near = r_ref[other, rows_of(group)]
            if group == 6:
                near = jnp.where(keep == (0 if part == 1 else 3), near, 0.0)
            total = total + near
        return total

    for chip in range(CHIPS):
        for part in range(4):
            top = gathered(chip, part, lambda g: slice(8 * g, 8 * g + 8), a)
            wet = gathered(chip, part, lambda g: slice(56 + g, 57 + g), a[:1])
            m = top * (1.0 / jnp.maximum(wet, FLOOR))
            u = jnp.broadcast_to(m[0:1], (8, 128))
            v = jnp.broadcast_to(m[1:2], (8, 128))
            t = jnp.broadcast_to(m[2:3], (8, 128))
            left = jnp.where(row < 3, 0.0, jnp.where((row == 5) | (row == 7), v, u))
            right = jnp.where(row == 3, u, jnp.where(row < 6, v, t))
            ti = 4 * chip + part
            q_scr[8 * ti : 8 * ti + 8] = m - left * right

    for block in range(8):
        x = [q_scr[pl.ds(64 * block + q, 8, stride=8), :] for q in range(8)]
        for k in range(3):
            for i in range(8):
                if not i & (1 << k):
                    j = i | (1 << k)
                    x[i], x[j] = swap_bit(x[i], x[j], lane, 16 << k)
        rows = jnp.concatenate(x, axis=0)
        table[64 * block : 64 * block + 64] = jnp.concatenate(three_parts(rows)[:2], axis=1)

    for m in range(4):
        here = slice(256 * m, 256 * m + 256)
        picked = dot(pick_ref[here], table[...])
        out_ref[here] = picked[:, :128] + picked[:, 128:]


def collect_call(blocks, pick):
    inside = pl.BlockSpec(memory_space=pltpu.VMEM)
    return pl.pallas_call(
        collect_kernel,
        out_shape=jax.ShapeDtypeStruct((pick.shape[0], 128), jnp.float32),
        in_specs=[inside] * 2,
        out_specs=inside,
        scratch_shapes=[
            pltpu.VMEM((512, 128), jnp.float32),
            pltpu.VMEM((512, 256), jnp.bfloat16),
        ],
        compiler_params=pltpu.CompilerParams(vmem_limit_bytes=COLLECT_VMEM),
        name="collect",
    )(blocks, pick)


def pick_matrix(patch, tally):
    ranks, capacity = patch.shape
    place = (patch // 64) * 64 + (patch % 8) * 8 + (patch // 8) % 8
    kept = jnp.arange(capacity)[None, :] < tally[:, None]
    place = jnp.where(kept, place, -1).reshape(ranks * capacity, 1)
    return (place == jnp.arange(512)[None, :]).astype(jnp.bfloat16)


def on_device(
    zonal_current_grid,
    meridional_current_grid,
    thermal_anomaly,
    water_indicator,
    owner_slot_patch_number,
    owner_slot_tally,
):
    ranks, capacity = owner_slot_patch_number.shape[1:]
    mine, theirs = filter_call(zonal_current_grid[0], meridional_current_grid[0], thermal_anomaly[0], water_indicator[0])
    theirs = lax.ppermute(theirs, "strip", [(i, i ^ 1) for i in range(STRIPS)])
    blocks = merge_call(mine, theirs)
    pick = pick_matrix(owner_slot_patch_number[0], owner_slot_tally[0])
    blocks, pick = lax.optimization_barrier((blocks, pick))
    same_core = [list(range(core, STRIPS, 2)) for core in range(2)]
    blocks = lax.all_to_all(blocks, "strip", split_axis=0, concat_axis=0, axis_index_groups=same_core, tiled=True)
    outgoing = collect_call(blocks, pick).reshape(ranks, capacity, 128)
    arrived = lax.all_to_all(outgoing, ("lev", "strip"), split_axis=0, concat_axis=0, tiled=True)
    return arrived.reshape(ranks * capacity, 128)


def solution(mesh):
    return jax.shard_map(
        on_device,
        mesh=mesh,
        in_specs=(
            P("lev", "strip", None),
            P("lev", "strip", None),
            P("lev", "strip", None),
            P("lev", "strip", None),
            P(("lev", "strip"), None, None),
            P(("lev", "strip"), None),
        ),
        out_specs=P(("lev", "strip"), None),
        check_vma=False,
    )
```

```python
import jax
import jax.numpy as jnp
import ml_dtypes
import numpy as np
from jax import lax
from jax.experimental import pallas as pl
from jax.experimental.pallas import tpu as pltpu
from jax.sharding import PartitionSpec as P

HALF = 20
SPREAD = 7.0
FLOOR = 0.05
ROWS = 32
COLS = 4096
STRIPS = 32
GROUPS = 5
SLAB = 48
CHIPS = 16
MERGED = 64
QUADS = 8
ENDS = (1, 8)
FILTER_VMEM = 24 * 1024 * 1024
COLLECT_VMEM = 16 * 1024 * 1024


def band(offsets):
    taps = np.arange(-HALF, HALF + 1).astype(np.float64)
    total = np.exp(-taps * taps / (2.0 * SPREAD * SPREAD)).sum()
    off = offsets.astype(np.float64)
    weights = np.exp(-off * off / (2.0 * SPREAD * SPREAD)) / total
    return np.where(np.abs(offsets) <= HALF, weights, 0.0).astype(np.float32)


def two_parts(matrix):
    high = matrix.astype(ml_dtypes.bfloat16)
    low = (matrix - high.astype(np.float32)).astype(ml_dtypes.bfloat16)
    return high, low


def zonal_matrices():
    lane = np.arange(128)
    strip = (lane // 4) % 4
    target = strip * 128 + 4 * (4 * (lane // 16) + lane % 4)
    source = np.arange(256)[:, None]
    left = band(source - np.where(strip == 3, target - 512, target)[None, :])
    right = band(source + 256 - np.where(strip == 0, target + 512, target)[None, :])
    return [np.concatenate(two_parts(m), axis=1) for m in (left, right)]


def partial_row(a, g):
    if g < 4:
        return 4 * (g - 1) + a
    return {0: 12, 3: -5}.get(a)


def meridional_matrices():
    rows = np.arange(ROWS)
    full = np.zeros((4 * GROUPS * 8, 8 * ROWS), np.float32)
    wet = np.zeros((4 * 8, ROWS), np.float32)
    for a in range(4):
        for g in range(GROUPS):
            i = partial_row(a, g)
            if i is None:
                continue
            weights = band(4 * i - rows)
            wet[a * 8 + g] = weights
            for p in range(8):
                full[(a * GROUPS + g) * 8 + p, p * ROWS : (p + 1) * ROWS] = weights
    return [np.concatenate(two_parts(m), axis=1) for m in (full, wet)]


def three_parts(x):
    first = x.astype(jnp.bfloat16)
    rest = x - first.astype(jnp.float32)
    second = rest.astype(jnp.bfloat16)
    third = (rest - second.astype(jnp.float32)).astype(jnp.bfloat16)
    return first, second, third


def dot(a, b):
    return jnp.dot(a, b, preferred_element_type=jnp.float32)


def swap_bit(zero, one, lane, stride):
    bit = (lane & stride) != 0
    return (
        jnp.where(bit, pltpu.roll(one, stride, 1), zero),
        jnp.where(bit, one, pltpu.roll(zero, 128 - stride, 1)),
    )


def filter_kernel(*refs):
    inputs, constants, outs = refs[:4], refs[4:8], refs[8:10]
    held, consts, (parts, left, right) = refs[10:14], refs[14:18], refs[18:21]
    in_sems, const_sems = refs[21:]
    is_first = lax.rem(lax.axis_index("strip"), 2) == 0
    wl_ref, wr_ref, gm_ref, gw_ref = consts

    loads = {}
    starts = (0,) + ENDS[:-1]
    for c, (begin, end) in enumerate(zip(starts, ENDS)):
        here = pl.ds(512 * begin, 512 * (end - begin))
        for k in range(4):
            loads[c, k] = pltpu.make_async_copy(inputs[k].at[:, here], held[k].at[:, here], in_sems.at[k, c])
            loads[c, k].start()
        if c == 0:
            fixed = [pltpu.make_async_copy(a, b, const_sems.at[n]) for n, (a, b) in enumerate(zip(constants, consts))]
            for copy in fixed:
                copy.start()

    def make_planes(c):
        for strip in range(4 * starts[c], 4 * ENDS[c]):
            here = slice(128 * strip, 128 * strip + 128)
            u, v, t = [held[k][:, here] for k in range(3)]
            w = held[3][:, here].astype(jnp.float32)
            wu, wv, wt = w * u, w * v, w * t
            fields = (wu, wv, wt, wu * u, wu * v, wv * v, wu * t, wv * t)
            for p, field in enumerate(fields):
                for n, part in enumerate(three_parts(field)[: 3 if p < 3 else 2]):
                    parts[n, p * ROWS : (p + 1) * ROWS, here] = part
            parts[0, 8 * ROWS :, here] = w.astype(jnp.bfloat16)

    def zonal(quads):
        for w_ref, start, to in ((wl_ref, 0, left), (wr_ref, 256, right)):
            w = w_ref[...]

            def stacked(n, rows, w):
                x = [parts[n, :rows, 512 * q + start : 512 * q + start + 256] for q in quads]
                return dot(jnp.concatenate(x, axis=0), w).reshape(len(quads), rows, -1)

            first = stacked(0, 9 * ROWS, w)
            second = stacked(1, 8 * ROWS, w)
            third = stacked(2, 3 * ROWS, w[:, :128])
            for n, q in enumerate(quads):
                z = first[n, : 8 * ROWS] + second[n]
                z = z[:, :128] + z[:, 128:]
                to[q, : 3 * ROWS] = z[: 3 * ROWS] + third[n]
                to[q, 3 * ROWS : 8 * ROWS] = z[3 * ROWS :]
                to[q, 8 * ROWS :] = first[n, 8 * ROWS :, :128] + first[n, 8 * ROWS :, 128:]

    lane = lax.broadcasted_iota(jnp.int32, (SLAB, 128), 1)
    strip_of_lane = (lax.broadcasted_iota(jnp.int32, (9 * ROWS, 128), 1) // 4) % 4

    def meridional(pair):
        z = []
        for q in pair:
            from_left = jnp.where(strip_of_lane == 3, left[(q + 1) % QUADS], left[q])
            from_right = jnp.where(strip_of_lane == 0, right[(q - 1) % QUADS], right[q])
            z.append(from_left + from_right)
        z = jnp.concatenate(z, axis=1)

        def across(g_ref, x):
            first, second, third = three_parts(x)
            depth = x.shape[0]
            high, low = g_ref[:, :depth], g_ref[:, depth:]
            return dot(high, third) + dot(low, first) + dot(high, second) + dot(high, first)

        y = across(gm_ref, z[: 8 * ROWS])
        yw = across(gw_ref, z[8 * ROWS :])
        for n, q in enumerate(pair):
            here = slice(128 * n, 128 * n + 128)
            x = [
                jnp.concatenate([y[40 * a : 40 * a + 40, here], yw[8 * a : 8 * a + 8, here]], axis=0)
                for a in range(4)
            ]
            x[0], x[1] = swap_bit(x[0], x[1], lane, 4)
            x[2], x[3] = swap_bit(x[2], x[3], lane, 4)
            x[0], x[2] = swap_bit(x[0], x[2], lane, 8)
            x[1], x[3] = swap_bit(x[1], x[3], lane, 8)
            for n in range(2):
                outs[0][2 * q + n] = jnp.where(is_first, x[2 * n], x[2 * n + 1])
                outs[1][2 * q + n] = jnp.where(is_first, x[2 * n + 1], x[2 * n])

    ready = 1
    for c, (begin, end) in enumerate(zip(starts, ENDS)):
        for k in range(4):
            loads[c, k].wait()
        make_planes(c)
        if c == 0:
            for copy in fixed:
                copy.wait()
        for q in range(begin, end, 4):
            zonal(range(q, min(q + 4, end)))
        while ready + 2 < end:
            meridional((ready, ready + 1))
            ready += 2
    meridional((7, 0))


def filter_call(u, v, t, w):
    constants = zonal_matrices() + meridional_matrices()
    anywhere = pl.BlockSpec(memory_space=pl.ANY)
    u, v, t, w, *constants = [
        pltpu.with_memory_space_constraint(jnp.asarray(x), pltpu.HBM) for x in (u, v, t, w, *constants)
    ]
    return pl.pallas_call(
        filter_kernel,
        out_shape=[jax.ShapeDtypeStruct((CHIPS, SLAB, 128), jnp.float32)] * 2,
        in_specs=[anywhere] * 8,
        out_specs=[pl.BlockSpec(memory_space=pltpu.VMEM)] * 2,
        scratch_shapes=[pltpu.VMEM((ROWS, COLS), x.dtype) for x in (u, v, t, w)]
        + [pltpu.VMEM(x.shape, jnp.bfloat16) for x in constants]
        + [
            pltpu.VMEM((3, 9 * ROWS, COLS), jnp.bfloat16),
            pltpu.VMEM((QUADS, 9 * ROWS, 128), jnp.float32),
            pltpu.VMEM((QUADS, 9 * ROWS, 128), jnp.float32),
            pltpu.SemaphoreType.DMA((4, len(ENDS))),
            pltpu.SemaphoreType.DMA((4,)),
        ],
        compiler_params=pltpu.CompilerParams(vmem_limit_bytes=FILTER_VMEM),
        name="filter",
    )(u, v, t, w, *constants)


def lane_rows():
    return (lax.broadcasted_iota(jnp.int32, (8, 128), 1) // 4) % 4


def merge_kernel(mine, theirs, out):
    is_first = lax.rem(lax.axis_index("strip"), 2) == 0
    a = lane_rows()
    for chip in range(CHIPS):
        for rows, to, keep in ((lambda g: slice(8 * g, 8 * g + 8), 0, a), (lambda g: slice(40 + g, 41 + g), 56, a[:1])):
            x = [mine[chip, rows(g)] for g in range(GROUPS)]
            y = [theirs[chip, rows(g)] for g in range(GROUPS)]
            one = [jnp.where(is_first, p, q) for p, q in zip(x, y)]
            two = [jnp.where(is_first, q, p) for p, q in zip(x, y)]
            groups = (
                one[0],
                one[1] + jnp.where(keep == 3, two[4], 0.0),
                one[2] + two[0],
                one[3] + two[1],
                two[2] + jnp.where(keep == 0, one[4], 0.0),
                two[3],
                jnp.where(keep == 3, one[4], two[4] * jnp.where(keep == 0, 1.0, 0.0)),
            )
            for g, group in enumerate(groups):
                if to == 0:
                    out[chip, 8 * g : 8 * g + 8] = group
                else:
                    out[chip, to + g : to + g + 1] = group
        out[chip, MERGED - 1 : MERGED] = jnp.zeros((1, 128), jnp.float32)


def merge_call(mine, theirs):
    inside = pl.BlockSpec(memory_space=pltpu.VMEM)
    return pl.pallas_call(
        merge_kernel,
        out_shape=jax.ShapeDtypeStruct((CHIPS, MERGED, 128), jnp.float32),
        in_specs=[inside] * 2,
        out_specs=inside,
        compiler_params=pltpu.CompilerParams(vmem_limit_bytes=COLLECT_VMEM),
        name="merge",
    )(mine, theirs)


def collect_kernel(r_ref, pick_ref, out_ref, q_scr, table):
    row = lax.broadcasted_iota(jnp.int32, (8, 128), 0)
    lane = lax.broadcasted_iota(jnp.int32, (8, 128), 1)
    a = lane_rows()

    def gathered(chip, part, rows_of, keep):
        total = r_ref[chip, rows_of(1 + part)]
        other = chip - 1 if part < 2 else chip + 1
        if 0 <= other < CHIPS:
            group = (5, 6, 6, 0)[part]
            near = r_ref[other, rows_of(group)]
            if group == 6:
                near = jnp.where(keep == (0 if part == 1 else 3), near, 0.0)
            total = total + near
        return total

    for chip in range(CHIPS):
        for part in range(4):
            top = gathered(chip, part, lambda g: slice(8 * g, 8 * g + 8), a)
            wet = gathered(chip, part, lambda g: slice(56 + g, 57 + g), a[:1])
            m = top * (1.0 / jnp.maximum(wet, FLOOR))
            u = jnp.broadcast_to(m[0:1], (8, 128))
            v = jnp.broadcast_to(m[1:2], (8, 128))
            t = jnp.broadcast_to(m[2:3], (8, 128))
            left = jnp.where(row < 3, 0.0, jnp.where((row == 5) | (row == 7), v, u))
            right = jnp.where(row == 3, u, jnp.where(row < 6, v, t))
            ti = 4 * chip + part
            q_scr[8 * ti : 8 * ti + 8] = m - left * right

    for block in range(8):
        x = [q_scr[pl.ds(64 * block + q, 8, stride=8), :] for q in range(8)]
        for k in range(3):
            for i in range(8):
                if not i & (1 << k):
                    j = i | (1 << k)
                    x[i], x[j] = swap_bit(x[i], x[j], lane, 16 << k)
        rows = jnp.concatenate(x, axis=0)
        table[64 * block : 64 * block + 64] = jnp.concatenate(three_parts(rows)[:2], axis=1)

    for m in range(4):
        here = slice(256 * m, 256 * m + 256)
        picked = dot(pick_ref[here], table[...])
        out_ref[here] = picked[:, :128] + picked[:, 128:]


def collect_call(blocks, pick):
    inside = pl.BlockSpec(memory_space=pltpu.VMEM)
    return pl.pallas_call(
        collect_kernel,
        out_shape=jax.ShapeDtypeStruct((pick.shape[0], 128), jnp.float32),
        in_specs=[inside] * 2,
        out_specs=inside,
        scratch_shapes=[
            pltpu.VMEM((512, 128), jnp.float32),
            pltpu.VMEM((512, 256), jnp.bfloat16),
        ],
        compiler_params=pltpu.CompilerParams(vmem_limit_bytes=COLLECT_VMEM),
        name="collect",
    )(blocks, pick)


def pick_matrix(patch, tally):
    ranks, capacity = patch.shape
    place = (patch // 64) * 64 + (patch % 8) * 8 + (patch // 8) % 8
    kept = jnp.arange(capacity)[None, :] < tally[:, None]
    place = jnp.where(kept, place, -1).reshape(ranks * capacity, 1)
    return (place == jnp.arange(512)[None, :]).astype(jnp.bfloat16)


def on_device(
    zonal_current_grid,
    meridional_current_grid,
    thermal_anomaly,
    water_indicator,
    owner_slot_patch_number,
    owner_slot_tally,
):
    ranks, capacity = owner_slot_patch_number.shape[1:]
    mine, theirs = filter_call(zonal_current_grid[0], meridional_current_grid[0], thermal_anomaly[0], water_indicator[0])
    theirs = lax.ppermute(theirs, "strip", [(i, i ^ 1) for i in range(STRIPS)])
    blocks = merge_call(mine, theirs)
    pick = pick_matrix(owner_slot_patch_number[0], owner_slot_tally[0])
    blocks, pick = lax.optimization_barrier((blocks, pick))
    same_core = [list(range(core, STRIPS, 2)) for core in range(2)]
    blocks = lax.all_to_all(blocks, "strip", split_axis=0, concat_axis=0, axis_index_groups=same_core, tiled=True)
    outgoing = collect_call(blocks, pick).reshape(ranks, capacity, 128)
    arrived = lax.all_to_all(outgoing, ("lev", "strip"), split_axis=0, concat_axis=0, tiled=True)
    return arrived.reshape(ranks * capacity, 128)


def solution(mesh):
    return jax.shard_map(
        on_device,
        mesh=mesh,
        in_specs=(
            P("lev", "strip", None),
            P("lev", "strip", None),
            P("lev", "strip", None),
            P("lev", "strip", None),
            P(("lev", "strip"), None, None),
            P(("lev", "strip"), None),
        ),
        out_specs=P(("lev", "strip"), None),
        check_vma=False,
    )
```

```python
import jax
import jax.numpy as jnp
import ml_dtypes
import numpy as np
from jax import lax
from jax.experimental import pallas as pl
from jax.experimental.pallas import tpu as pltpu
from jax.sharding import PartitionSpec as P

HALF = 20
SPREAD = 7.0
FLOOR = 0.05
ROWS = 32
COLS = 4096
STRIPS = 32
GROUPS = 5
SLAB = 48
CHIPS = 16
ORDER = [4 * y + (x if y % 2 == 0 else 3 - x) for y in range(4) for x in range(4)]
PLACE = [ORDER.index(chip) for chip in range(CHIPS)]
MERGED = 64
QUADS = 8
ENDS = (1, 8)
FILTER_VMEM = 24 * 1024 * 1024
COLLECT_VMEM = 16 * 1024 * 1024


def band(offsets):
    taps = np.arange(-HALF, HALF + 1).astype(np.float64)
    total = np.exp(-taps * taps / (2.0 * SPREAD * SPREAD)).sum()
    off = offsets.astype(np.float64)
    weights = np.exp(-off * off / (2.0 * SPREAD * SPREAD)) / total
    return np.where(np.abs(offsets) <= HALF, weights, 0.0).astype(np.float32)


def two_parts(matrix):
    high = matrix.astype(ml_dtypes.bfloat16)
    low = (matrix - high.astype(np.float32)).astype(ml_dtypes.bfloat16)
    return high, low


def zonal_matrices():
    lane = np.arange(128)
    strip = (lane // 4) % 4
    target = strip * 128 + 4 * (4 * (lane // 16) + lane % 4)
    source = np.arange(256)[:, None]
    left = band(source - np.where(strip == 3, target - 512, target)[None, :])
    right = band(source + 256 - np.where(strip == 0, target + 512, target)[None, :])
    return [np.concatenate(two_parts(m), axis=1) for m in (left, right)]


def partial_row(a, g):
    if g < 4:
        return 4 * (g - 1) + a
    return {0: 12, 3: -5}.get(a)


def meridional_matrices():
    rows = np.arange(ROWS)
    full = np.zeros((4 * GROUPS * 8, 8 * ROWS), np.float32)
    wet = np.zeros((4 * 8, ROWS), np.float32)
    for a in range(4):
        for g in range(GROUPS):
            i = partial_row(a, g)
            if i is None:
                continue
            weights = band(4 * i - rows)
            wet[a * 8 + g] = weights
            for p in range(8):
                full[(a * GROUPS + g) * 8 + p, p * ROWS : (p + 1) * ROWS] = weights
    return [np.concatenate(two_parts(m), axis=1) for m in (full, wet)]


def three_parts(x):
    first = x.astype(jnp.bfloat16)
    rest = x - first.astype(jnp.float32)
    second = rest.astype(jnp.bfloat16)
    third = (rest - second.astype(jnp.float32)).astype(jnp.bfloat16)
    return first, second, third


def dot(a, b):
    return jnp.dot(a, b, preferred_element_type=jnp.float32)


def swap_bit(zero, one, lane, stride):
    bit = (lane & stride) != 0
    return (
        jnp.where(bit, pltpu.roll(one, stride, 1), zero),
        jnp.where(bit, one, pltpu.roll(zero, 128 - stride, 1)),
    )


def filter_kernel(*refs):
    inputs, constants, outs = refs[:4], refs[4:8], refs[8:10]
    held, consts, (parts, left, right) = refs[10:14], refs[14:18], refs[18:21]
    in_sems, const_sems = refs[21:]
    is_first = lax.rem(lax.axis_index("strip"), 2) == 0
    wl_ref, wr_ref, gm_ref, gw_ref = consts

    loads = {}
    starts = (0,) + ENDS[:-1]
    for c, (begin, end) in enumerate(zip(starts, ENDS)):
        here = pl.ds(512 * begin, 512 * (end - begin))
        for k in range(4):
            loads[c, k] = pltpu.make_async_copy(inputs[k].at[:, here], held[k].at[:, here], in_sems.at[k, c])
            loads[c, k].start()
        if c == 0:
            fixed = [pltpu.make_async_copy(a, b, const_sems.at[n]) for n, (a, b) in enumerate(zip(constants, consts))]
            for copy in fixed:
                copy.start()

    def make_planes(c):
        for strip in range(4 * starts[c], 4 * ENDS[c]):
            here = slice(128 * strip, 128 * strip + 128)
            u, v, t = [held[k][:, here] for k in range(3)]
            w = held[3][:, here].astype(jnp.float32)
            wu, wv, wt = w * u, w * v, w * t
            fields = (wu, wv, wt, wu * u, wu * v, wv * v, wu * t, wv * t)
            for p, field in enumerate(fields):
                for n, part in enumerate(three_parts(field)[: 3 if p < 3 else 2]):
                    parts[n, p * ROWS : (p + 1) * ROWS, here] = part
            parts[0, 8 * ROWS :, here] = w.astype(jnp.bfloat16)

    def zonal(quads):
        for w_ref, start, to in ((wl_ref, 0, left), (wr_ref, 256, right)):
            w = w_ref[...]

            def stacked(n, rows, w):
                x = [parts[n, :rows, 512 * q + start : 512 * q + start + 256] for q in quads]
                return dot(jnp.concatenate(x, axis=0), w).reshape(len(quads), rows, -1)

            first = stacked(0, 9 * ROWS, w)
            second = stacked(1, 8 * ROWS, w)
            third = stacked(2, 3 * ROWS, w[:, :128])
            for n, q in enumerate(quads):
                z = first[n, : 8 * ROWS] + second[n]
                z = z[:, :128] + z[:, 128:]
                to[q, : 3 * ROWS] = z[: 3 * ROWS] + third[n]
                to[q, 3 * ROWS : 8 * ROWS] = z[3 * ROWS :]
                to[q, 8 * ROWS :] = first[n, 8 * ROWS :, :128] + first[n, 8 * ROWS :, 128:]

    lane = lax.broadcasted_iota(jnp.int32, (SLAB, 128), 1)
    strip_of_lane = (lax.broadcasted_iota(jnp.int32, (9 * ROWS, 128), 1) // 4) % 4

    def meridional(pair):
        z = []
        for q in pair:
            from_left = jnp.where(strip_of_lane == 3, left[(q + 1) % QUADS], left[q])
            from_right = jnp.where(strip_of_lane == 0, right[(q - 1) % QUADS], right[q])
            z.append(from_left + from_right)
        z = jnp.concatenate(z, axis=1)

        def across(g_ref, x):
            first, second, third = three_parts(x)
            depth = x.shape[0]
            high, low = g_ref[:, :depth], g_ref[:, depth:]
            return dot(high, third) + dot(low, first) + dot(high, second) + dot(high, first)

        y = across(gm_ref, z[: 8 * ROWS])
        yw = across(gw_ref, z[8 * ROWS :])
        for n, q in enumerate(pair):
            here = slice(128 * n, 128 * n + 128)
            x = [
                jnp.concatenate([y[40 * a : 40 * a + 40, here], yw[8 * a : 8 * a + 8, here]], axis=0)
                for a in range(4)
            ]
            x[0], x[1] = swap_bit(x[0], x[1], lane, 4)
            x[2], x[3] = swap_bit(x[2], x[3], lane, 4)
            x[0], x[2] = swap_bit(x[0], x[2], lane, 8)
            x[1], x[3] = swap_bit(x[1], x[3], lane, 8)
            for n in range(2):
                outs[0][2 * q + n] = jnp.where(is_first, x[2 * n], x[2 * n + 1])
                outs[1][2 * q + n] = jnp.where(is_first, x[2 * n + 1], x[2 * n])

    ready = 1
    for c, (begin, end) in enumerate(zip(starts, ENDS)):
        for k in range(4):
            loads[c, k].wait()
        make_planes(c)
        if c == 0:
            for copy in fixed:
                copy.wait()
        for q in range(begin, end, 4):
            zonal(range(q, min(q + 4, end)))
        while ready + 2 < end:
            meridional((ready, ready + 1))
            ready += 2
    meridional((7, 0))


def filter_call(u, v, t, w):
    constants = zonal_matrices() + meridional_matrices()
    anywhere = pl.BlockSpec(memory_space=pl.ANY)
    u, v, t, w, *constants = [
        pltpu.with_memory_space_constraint(jnp.asarray(x), pltpu.HBM) for x in (u, v, t, w, *constants)
    ]
    return pl.pallas_call(
        filter_kernel,
        out_shape=[jax.ShapeDtypeStruct((CHIPS, SLAB, 128), jnp.float32)] * 2,
        in_specs=[anywhere] * 8,
        out_specs=[pl.BlockSpec(memory_space=pltpu.VMEM)] * 2,
        scratch_shapes=[pltpu.VMEM((ROWS, COLS), x.dtype) for x in (u, v, t, w)]
        + [pltpu.VMEM(x.shape, jnp.bfloat16) for x in constants]
        + [
            pltpu.VMEM((3, 9 * ROWS, COLS), jnp.bfloat16),
            pltpu.VMEM((QUADS, 9 * ROWS, 128), jnp.float32),
            pltpu.VMEM((QUADS, 9 * ROWS, 128), jnp.float32),
            pltpu.SemaphoreType.DMA((4, len(ENDS))),
            pltpu.SemaphoreType.DMA((4,)),
        ],
        compiler_params=pltpu.CompilerParams(vmem_limit_bytes=FILTER_VMEM),
        name="filter",
    )(u, v, t, w, *constants)


def lane_rows():
    return (lax.broadcasted_iota(jnp.int32, (8, 128), 1) // 4) % 4


def merge_kernel(mine, theirs, out):
    is_first = lax.rem(lax.axis_index("strip"), 2) == 0
    a = lane_rows()
    for chip in range(CHIPS):
        for rows, to, keep in ((lambda g: slice(8 * g, 8 * g + 8), 0, a), (lambda g: slice(40 + g, 41 + g), 56, a[:1])):
            x = [mine[chip, rows(g)] for g in range(GROUPS)]
            y = [theirs[chip, rows(g)] for g in range(GROUPS)]
            one = [jnp.where(is_first, p, q) for p, q in zip(x, y)]
            two = [jnp.where(is_first, q, p) for p, q in zip(x, y)]
            groups = (
                one[0],
                one[1] + jnp.where(keep == 3, two[4], 0.0),
                one[2] + two[0],
                one[3] + two[1],
                two[2] + jnp.where(keep == 0, one[4], 0.0),
                two[3],
                jnp.where(keep == 3, one[4], two[4] * jnp.where(keep == 0, 1.0, 0.0)),
            )
            for g, group in enumerate(groups):
                if to == 0:
                    out[PLACE[chip], 8 * g : 8 * g + 8] = group
                else:
                    out[PLACE[chip], to + g : to + g + 1] = group
        out[PLACE[chip], MERGED - 1 : MERGED] = jnp.zeros((1, 128), jnp.float32)


def merge_call(mine, theirs):
    inside = pl.BlockSpec(memory_space=pltpu.VMEM)
    return pl.pallas_call(
        merge_kernel,
        out_shape=jax.ShapeDtypeStruct((CHIPS, MERGED, 128), jnp.float32),
        in_specs=[inside] * 2,
        out_specs=inside,
        compiler_params=pltpu.CompilerParams(vmem_limit_bytes=COLLECT_VMEM),
        name="merge",
    )(mine, theirs)


def collect_kernel(r_ref, pick_ref, out_ref, q_scr, table):
    row = lax.broadcasted_iota(jnp.int32, (8, 128), 0)
    lane = lax.broadcasted_iota(jnp.int32, (8, 128), 1)
    a = lane_rows()

    def gathered(chip, part, rows_of, keep):
        total = r_ref[PLACE[chip], rows_of(1 + part)]
        other = chip - 1 if part < 2 else chip + 1
        if 0 <= other < CHIPS:
            group = (5, 6, 6, 0)[part]
            near = r_ref[PLACE[other], rows_of(group)]
            if group == 6:
                near = jnp.where(keep == (0 if part == 1 else 3), near, 0.0)
            total = total + near
        return total

    for chip in range(CHIPS):
        for part in range(4):
            top = gathered(chip, part, lambda g: slice(8 * g, 8 * g + 8), a)
            wet = gathered(chip, part, lambda g: slice(56 + g, 57 + g), a[:1])
            m = top * (1.0 / jnp.maximum(wet, FLOOR))
            u = jnp.broadcast_to(m[0:1], (8, 128))
            v = jnp.broadcast_to(m[1:2], (8, 128))
            t = jnp.broadcast_to(m[2:3], (8, 128))
            left = jnp.where(row < 3, 0.0, jnp.where((row == 5) | (row == 7), v, u))
            right = jnp.where(row == 3, u, jnp.where(row < 6, v, t))
            ti = 4 * chip + part
            q_scr[8 * ti : 8 * ti + 8] = m - left * right

    for block in range(8):
        x = [q_scr[pl.ds(64 * block + q, 8, stride=8), :] for q in range(8)]
        for k in range(3):
            for i in range(8):
                if not i & (1 << k):
                    j = i | (1 << k)
                    x[i], x[j] = swap_bit(x[i], x[j], lane, 16 << k)
        rows = jnp.concatenate(x, axis=0)
        table[64 * block : 64 * block + 64] = jnp.concatenate(three_parts(rows)[:2], axis=1)

    for m in range(4):
        here = slice(256 * m, 256 * m + 256)
        picked = dot(pick_ref[here], table[...])
        out_ref[here] = picked[:, :128] + picked[:, 128:]


def collect_call(blocks, pick):
    inside = pl.BlockSpec(memory_space=pltpu.VMEM)
    return pl.pallas_call(
        collect_kernel,
        out_shape=jax.ShapeDtypeStruct((pick.shape[0], 128), jnp.float32),
        in_specs=[inside] * 2,
        out_specs=inside,
        scratch_shapes=[
            pltpu.VMEM((512, 128), jnp.float32),
            pltpu.VMEM((512, 256), jnp.bfloat16),
        ],
        compiler_params=pltpu.CompilerParams(vmem_limit_bytes=COLLECT_VMEM),
        name="collect",
    )(blocks, pick)


def pick_matrix(patch, tally):
    ranks, capacity = patch.shape
    place = (patch // 64) * 64 + (patch % 8) * 8 + (patch // 8) % 8
    kept = jnp.arange(capacity)[None, :] < tally[:, None]
    place = jnp.where(kept, place, -1).reshape(ranks * capacity, 1)
    return (place == jnp.arange(512)[None, :]).astype(jnp.bfloat16)


def on_device(
    zonal_current_grid,
    meridional_current_grid,
    thermal_anomaly,
    water_indicator,
    owner_slot_patch_number,
    owner_slot_tally,
):
    ranks, capacity = owner_slot_patch_number.shape[1:]
    mine, theirs = filter_call(zonal_current_grid[0], meridional_current_grid[0], thermal_anomaly[0], water_indicator[0])
    theirs = lax.ppermute(theirs, "strip", [(i, i ^ 1) for i in range(STRIPS)])
    blocks = merge_call(mine, theirs)
    pick = pick_matrix(owner_slot_patch_number[0], owner_slot_tally[0])
    blocks, pick = lax.optimization_barrier((blocks, pick))
    same_core = [[2 * chip + core for chip in ORDER] for core in range(2)]
    blocks = lax.all_to_all(blocks, "strip", split_axis=0, concat_axis=0, axis_index_groups=same_core, tiled=True)
    outgoing = collect_call(blocks, pick).reshape(ranks, capacity, 128)
    arrived = lax.all_to_all(outgoing, ("lev", "strip"), split_axis=0, concat_axis=0, tiled=True)
    return arrived.reshape(ranks * capacity, 128)


def solution(mesh):
    return jax.shard_map(
        on_device,
        mesh=mesh,
        in_specs=(
            P("lev", "strip", None),
            P("lev", "strip", None),
            P("lev", "strip", None),
            P("lev", "strip", None),
            P(("lev", "strip"), None, None),
            P(("lev", "strip"), None),
        ),
        out_specs=P(("lev", "strip"), None),
        check_vma=False,
    )
```

```python
import jax
import jax.numpy as jnp
import ml_dtypes
import numpy as np
from jax import lax
from jax.experimental import pallas as pl
from jax.experimental.pallas import tpu as pltpu
from jax.sharding import PartitionSpec as P

HALF = 20
SPREAD = 7.0
FLOOR = 0.05
ROWS = 32
COLS = 4096
STRIPS = 32
GROUPS = 5
SLAB = 48
CHIPS = 16
MERGED = 64
QUADS = 8
ENDS = (2, 8)
FILTER_VMEM = 24 * 1024 * 1024
COLLECT_VMEM = 16 * 1024 * 1024


def band(offsets):
    taps = np.arange(-HALF, HALF + 1).astype(np.float64)
    total = np.exp(-taps * taps / (2.0 * SPREAD * SPREAD)).sum()
    off = offsets.astype(np.float64)
    weights = np.exp(-off * off / (2.0 * SPREAD * SPREAD)) / total
    return np.where(np.abs(offsets) <= HALF, weights, 0.0).astype(np.float32)


def two_parts(matrix):
    high = matrix.astype(ml_dtypes.bfloat16)
    low = (matrix - high.astype(np.float32)).astype(ml_dtypes.bfloat16)
    return high, low


def zonal_matrices():
    lane = np.arange(128)
    strip = (lane // 4) % 4
    target = strip * 128 + 4 * (4 * (lane // 16) + lane % 4)
    source = np.arange(256)[:, None]
    left = band(source - np.where(strip == 3, target - 512, target)[None, :])
    right = band(source + 256 - np.where(strip == 0, target + 512, target)[None, :])
    return [np.concatenate(two_parts(m), axis=1) for m in (left, right)]


def partial_row(a, g):
    if g < 4:
        return 4 * (g - 1) + a
    return {0: 12, 3: -5}.get(a)


def meridional_matrices():
    rows = np.arange(ROWS)
    full = np.zeros((4 * GROUPS * 8, 8 * ROWS), np.float32)
    wet = np.zeros((4 * 8, ROWS), np.float32)
    for a in range(4):
        for g in range(GROUPS):
            i = partial_row(a, g)
            if i is None:
                continue
            weights = band(4 * i - rows)
            wet[a * 8 + g] = weights
            for p in range(8):
                full[(a * GROUPS + g) * 8 + p, p * ROWS : (p + 1) * ROWS] = weights
    return [np.concatenate(two_parts(m), axis=1) for m in (full, wet)]


def three_parts(x):
    first = x.astype(jnp.bfloat16)
    rest = x - first.astype(jnp.float32)
    second = rest.astype(jnp.bfloat16)
    third = (rest - second.astype(jnp.float32)).astype(jnp.bfloat16)
    return first, second, third


def dot(a, b):
    return jnp.dot(a, b, preferred_element_type=jnp.float32)


def swap_bit(zero, one, lane, stride):
    bit = (lane & stride) != 0
    return (
        jnp.where(bit, pltpu.roll(one, stride, 1), zero),
        jnp.where(bit, one, pltpu.roll(zero, 128 - stride, 1)),
    )


def filter_kernel(*refs):
    inputs, constants, outs = refs[:4], refs[4:8], refs[8:10]
    held, consts, (parts, left, right) = refs[10:14], refs[14:18], refs[18:21]
    in_sems, const_sems = refs[21:]
    is_first = lax.rem(lax.axis_index("strip"), 2) == 0
    wl_ref, wr_ref, gm_ref, gw_ref = consts

    loads = {}
    starts = (0,) + ENDS[:-1]
    for c, (begin, end) in enumerate(zip(starts, ENDS)):
        here = pl.ds(512 * begin, 512 * (end - begin))
        for k in range(4):
            loads[c, k] = pltpu.make_async_copy(inputs[k].at[:, here], held[k].at[:, here], in_sems.at[k, c])
            loads[c, k].start()
        if c == 0:
            fixed = [pltpu.make_async_copy(a, b, const_sems.at[n]) for n, (a, b) in enumerate(zip(constants, consts))]
            for copy in fixed:
                copy.start()

    def make_planes(c):
        for strip in range(4 * starts[c], 4 * ENDS[c]):
            here = slice(128 * strip, 128 * strip + 128)
            u, v, t = [held[k][:, here] for k in range(3)]
            w = held[3][:, here].astype(jnp.float32)
            wu, wv, wt = w * u, w * v, w * t
            fields = (wu, wv, wt, wu * u, wu * v, wv * v, wu * t, wv * t)
            for p, field in enumerate(fields):
                for n, part in enumerate(three_parts(field)[: 3 if p < 3 else 2]):
                    parts[n, p * ROWS : (p + 1) * ROWS, here] = part
            parts[0, 8 * ROWS :, here] = w.astype(jnp.bfloat16)

    def zonal(quads):
        for w_ref, start, to in ((wl_ref, 0, left), (wr_ref, 256, right)):
            w = w_ref[...]

            def stacked(n, rows, w):
                x = [parts[n, :rows, 512 * q + start : 512 * q + start + 256] for q in quads]
                return dot(jnp.concatenate(x, axis=0), w).reshape(len(quads), rows, -1)

            first = stacked(0, 9 * ROWS, w)
            second = stacked(1, 8 * ROWS, w)
            third = stacked(2, 3 * ROWS, w[:, :128])
            for n, q in enumerate(quads):
                z = first[n, : 8 * ROWS] + second[n]
                z = z[:, :128] + z[:, 128:]
                to[q, : 3 * ROWS] = z[: 3 * ROWS] + third[n]
                to[q, 3 * ROWS : 8 * ROWS] = z[3 * ROWS :]
                to[q, 8 * ROWS :] = first[n, 8 * ROWS :, :128] + first[n, 8 * ROWS :, 128:]

    lane = lax.broadcasted_iota(jnp.int32, (SLAB, 128), 1)
    strip_of_lane = (lax.broadcasted_iota(jnp.int32, (9 * ROWS, 128), 1) // 4) % 4

    def meridional(pair):
        z = []
        for q in pair:
            from_left = jnp.where(strip_of_lane == 3, left[(q + 1) % QUADS], left[q])
            from_right = jnp.where(strip_of_lane == 0, right[(q - 1) % QUADS], right[q])
            z.append(from_left + from_right)
        z = jnp.concatenate(z, axis=1)

        def across(g_ref, x):
            first, second, third = three_parts(x)
            depth = x.shape[0]
            high, low = g_ref[:, :depth], g_ref[:, depth:]
            return dot(high, third) + dot(low, first) + dot(high, second) + dot(high, first)

        y = across(gm_ref, z[: 8 * ROWS])
        yw = across(gw_ref, z[8 * ROWS :])
        for n, q in enumerate(pair):
            here = slice(128 * n, 128 * n + 128)
            x = [
                jnp.concatenate([y[40 * a : 40 * a + 40, here], yw[8 * a : 8 * a + 8, here]], axis=0)
                for a in range(4)
            ]
            x[0], x[1] = swap_bit(x[0], x[1], lane, 4)
            x[2], x[3] = swap_bit(x[2], x[3], lane, 4)
            x[0], x[2] = swap_bit(x[0], x[2], lane, 8)
            x[1], x[3] = swap_bit(x[1], x[3], lane, 8)
            for n in range(2):
                outs[0][2 * q + n] = jnp.where(is_first, x[2 * n], x[2 * n + 1])
                outs[1][2 * q + n] = jnp.where(is_first, x[2 * n + 1], x[2 * n])

    ready = 1
    for c, (begin, end) in enumerate(zip(starts, ENDS)):
        for k in range(4):
            loads[c, k].wait()
        make_planes(c)
        if c == 0:
            for copy in fixed:
                copy.wait()
        for q in range(begin, end, 3):
            zonal(range(q, min(q + 3, end)))
        while ready + 2 < end:
            meridional((ready, ready + 1))
            ready += 2
    meridional((7, 0))


def filter_call(u, v, t, w):
    constants = zonal_matrices() + meridional_matrices()
    anywhere = pl.BlockSpec(memory_space=pl.ANY)
    u, v, t, w, *constants = [
        pltpu.with_memory_space_constraint(jnp.asarray(x), pltpu.HBM) for x in (u, v, t, w, *constants)
    ]
    return pl.pallas_call(
        filter_kernel,
        out_shape=[jax.ShapeDtypeStruct((CHIPS, SLAB, 128), jnp.float32)] * 2,
        in_specs=[anywhere] * 8,
        out_specs=[pl.BlockSpec(memory_space=pltpu.VMEM)] * 2,
        scratch_shapes=[pltpu.VMEM((ROWS, COLS), x.dtype) for x in (u, v, t, w)]
        + [pltpu.VMEM(x.shape, jnp.bfloat16) for x in constants]
        + [
            pltpu.VMEM((3, 9 * ROWS, COLS), jnp.bfloat16),
            pltpu.VMEM((QUADS, 9 * ROWS, 128), jnp.float32),
            pltpu.VMEM((QUADS, 9 * ROWS, 128), jnp.float32),
            pltpu.SemaphoreType.DMA((4, len(ENDS))),
            pltpu.SemaphoreType.DMA((4,)),
        ],
        compiler_params=pltpu.CompilerParams(vmem_limit_bytes=FILTER_VMEM),
        name="filter",
    )(u, v, t, w, *constants)


def lane_rows():
    return (lax.broadcasted_iota(jnp.int32, (8, 128), 1) // 4) % 4


def merge_kernel(mine, theirs, out):
    is_first = lax.rem(lax.axis_index("strip"), 2) == 0
    a = lane_rows()
    for chip in range(CHIPS):
        for rows, to, keep in ((lambda g: slice(8 * g, 8 * g + 8), 0, a), (lambda g: slice(40 + g, 41 + g), 56, a[:1])):
            x = [mine[chip, rows(g)] for g in range(GROUPS)]
            y = [theirs[chip, rows(g)] for g in range(GROUPS)]
            one = [jnp.where(is_first, p, q) for p, q in zip(x, y)]
            two = [jnp.where(is_first, q, p) for p, q in zip(x, y)]
            groups = (
                one[0],
                one[1] + jnp.where(keep == 3, two[4], 0.0),
                one[2] + two[0],
                one[3] + two[1],
                two[2] + jnp.where(keep == 0, one[4], 0.0),
                two[3],
                jnp.where(keep == 3, one[4], two[4] * jnp.where(keep == 0, 1.0, 0.0)),
            )
            for g, group in enumerate(groups):
                if to == 0:
                    out[chip, 8 * g : 8 * g + 8] = group
                else:
                    out[chip, to + g : to + g + 1] = group
        out[chip, MERGED - 1 : MERGED] = jnp.zeros((1, 128), jnp.float32)


def merge_call(mine, theirs):
    inside = pl.BlockSpec(memory_space=pltpu.VMEM)
    return pl.pallas_call(
        merge_kernel,
        out_shape=jax.ShapeDtypeStruct((CHIPS, MERGED, 128), jnp.float32),
        in_specs=[inside] * 2,
        out_specs=inside,
        compiler_params=pltpu.CompilerParams(vmem_limit_bytes=COLLECT_VMEM),
        name="merge",
    )(mine, theirs)


def collect_kernel(r_ref, pick_ref, out_ref, q_scr, table):
    row = lax.broadcasted_iota(jnp.int32, (8, 128), 0)
    lane = lax.broadcasted_iota(jnp.int32, (8, 128), 1)
    a = lane_rows()

    def gathered(chip, part, rows_of, keep):
        total = r_ref[chip, rows_of(1 + part)]
        other = chip - 1 if part < 2 else chip + 1
        if 0 <= other < CHIPS:
            group = (5, 6, 6, 0)[part]
            near = r_ref[other, rows_of(group)]
            if group == 6:
                near = jnp.where(keep == (0 if part == 1 else 3), near, 0.0)
            total = total + near
        return total

    for chip in range(CHIPS):
        for part in range(4):
            top = gathered(chip, part, lambda g: slice(8 * g, 8 * g + 8), a)
            wet = gathered(chip, part, lambda g: slice(56 + g, 57 + g), a[:1])
            m = top * (1.0 / jnp.maximum(wet, FLOOR))
            u = jnp.broadcast_to(m[0:1], (8, 128))
            v = jnp.broadcast_to(m[1:2], (8, 128))
            t = jnp.broadcast_to(m[2:3], (8, 128))
            left = jnp.where(row < 3, 0.0, jnp.where((row == 5) | (row == 7), v, u))
            right = jnp.where(row == 3, u, jnp.where(row < 6, v, t))
            ti = 4 * chip + part
            q_scr[8 * ti : 8 * ti + 8] = m - left * right

    for block in range(8):
        x = [q_scr[pl.ds(64 * block + q, 8, stride=8), :] for q in range(8)]
        for k in range(3):
            for i in range(8):
                if not i & (1 << k):
                    j = i | (1 << k)
                    x[i], x[j] = swap_bit(x[i], x[j], lane, 16 << k)
        rows = jnp.concatenate(x, axis=0)
        table[64 * block : 64 * block + 64] = jnp.concatenate(three_parts(rows)[:2], axis=1)

    for m in range(4):
        here = slice(256 * m, 256 * m + 256)
        picked = dot(pick_ref[here], table[...])
        out_ref[here] = picked[:, :128] + picked[:, 128:]


def collect_call(blocks, pick):
    inside = pl.BlockSpec(memory_space=pltpu.VMEM)
    return pl.pallas_call(
        collect_kernel,
        out_shape=jax.ShapeDtypeStruct((pick.shape[0], 128), jnp.float32),
        in_specs=[inside] * 2,
        out_specs=inside,
        scratch_shapes=[
            pltpu.VMEM((512, 128), jnp.float32),
            pltpu.VMEM((512, 256), jnp.bfloat16),
        ],
        compiler_params=pltpu.CompilerParams(vmem_limit_bytes=COLLECT_VMEM),
        name="collect",
    )(blocks, pick)


def pick_matrix(patch, tally):
    ranks, capacity = patch.shape
    place = (patch // 64) * 64 + (patch % 8) * 8 + (patch // 8) % 8
    kept = jnp.arange(capacity)[None, :] < tally[:, None]
    place = jnp.where(kept, place, -1).reshape(ranks * capacity, 1)
    return (place == jnp.arange(512)[None, :]).astype(jnp.bfloat16)


def on_device(
    zonal_current_grid,
    meridional_current_grid,
    thermal_anomaly,
    water_indicator,
    owner_slot_patch_number,
    owner_slot_tally,
):
    ranks, capacity = owner_slot_patch_number.shape[1:]
    mine, theirs = filter_call(zonal_current_grid[0], meridional_current_grid[0], thermal_anomaly[0], water_indicator[0])
    theirs = lax.ppermute(theirs, "strip", [(i, i ^ 1) for i in range(STRIPS)])
    blocks = merge_call(mine, theirs)
    pick = pick_matrix(owner_slot_patch_number[0], owner_slot_tally[0])
    blocks, pick = lax.optimization_barrier((blocks, pick))
    same_core = [list(range(core, STRIPS, 2)) for core in range(2)]
    blocks = lax.all_to_all(blocks, "strip", split_axis=0, concat_axis=0, axis_index_groups=same_core, tiled=True)
    outgoing = collect_call(blocks, pick).reshape(ranks, capacity, 128)
    arrived = lax.all_to_all(outgoing, ("lev", "strip"), split_axis=0, concat_axis=0, tiled=True)
    return arrived.reshape(ranks * capacity, 128)


def solution(mesh):
    return jax.shard_map(
        on_device,
        mesh=mesh,
        in_specs=(
            P("lev", "strip", None),
            P("lev", "strip", None),
            P("lev", "strip", None),
            P("lev", "strip", None),
            P(("lev", "strip"), None, None),
            P(("lev", "strip"), None),
        ),
        out_specs=P(("lev", "strip"), None),
        check_vma=False,
    )
```
